32 devices in a mesh: light: 4 (over y, x), view: 8 (over z, core).
Axes of the slice: x: 2, y: 2, z: 4, core: 2. Of those that a mesh axis runs over, the one named last changes fastest.
Arguments:
- density: float32 [32, 64, 2048], P('light', 'view'), may hold values from 0.1 to 2
- albedo: bfloat16 [3, 32, 64, 2048], P(None, 'light', 'view'), may hold values from 0.099609375 to 1
- light_color: float32 [8, 3], replicated, may hold values from 0.5 to 1.5
- light_shift: int32 [8], replicated, may hold values from -1 to 1
- view_flip: int32 [32], P('light'), may hold values 0 or 1
Outputs:
- images: float32 [8, 4, 65536], P(None, None, ('light', 'view'))
The draws below stay inside these ranges and needn't reach their ends.
Inputs may be any that keep to these rules, and one draw needn't show every extreme that they name: `light_shift`: every light steps sideways by at most one cell per slice. `view_flip`: 0 means lower view indices lie in front, 1 means higher ones do.
All inputs are finite; a program needn't handle non-finite values. No bound on the sum of `view_flip` on one device may be relied on, other than what follows from the above.
Results may differ from the reference program's by a relative error of at most 0.0003.
Values sent between devices are 32-bit elements; how exact they have to be, the bound alone decides.
A program may use at most 64 MiB of HBM per device.

```python
import math
import jax
import jax.numpy as jnp
from jax import lax

W = 2048
LIGHTS = 8
NX = 32
NY = 64


def set_ends(result, key, low, top_value):
    longest = result.shape.index(max(result.shape))
    spots = []
    for shift in (0, 1):
        where = [jax.random.randint(jax.random.fold_in(key, axis), (), 0, length) for axis, length in enumerate(result.shape)]
        where[longest] = (where[longest] + shift) % result.shape[longest]
        spots.append(tuple(where))
    return result.at[spots[0]].set(low).at[spots[1]].set(top_value)


def steps_of(own_key, extent, shards, low, largest):
    def one(position, parts):
        steps = jax.random.uniform(jax.random.fold_in(jax.random.fold_in(own_key, 6), position), (parts,), jnp.float32, low / len(shards), largest / len(shards))
        return jnp.repeat(jnp.exp(steps), extent[position] // parts).reshape((-1,) + (1,) * (len(extent) - position - 1))

    gain = one(*shards[0])
    for cut in shards[1:]:
        gain = gain * one(*cut)
    return gain


def setup_inputs(seed: int = 0) -> dict:
    keys = jax.random.split(jax.random.key(seed), 6)
    density = jnp.clip(jnp.exp(math.log(2.0) - 2.9957323 * jax.random.uniform(keys[0], (NX, NY, W), jnp.float32) ** steps_of(keys[0], (NX, NY, W), ((0, 4), (1, 8)), -0.2, 0.2)), 0.1, 2.0)
    albedo = jnp.clip(0.099609375 + 0.9003906 * jax.random.uniform(keys[1], (3, NX, NY, W), jnp.float32) ** steps_of(keys[1], (3, NX, NY, W), ((1, 4), (2, 8)), -0.2, 0.2), 0.099609375, 1.0).astype(jnp.bfloat16)
    light_color = jnp.clip(jax.random.uniform(keys[2], (LIGHTS, 3), jnp.float32, 0.5, 1.5), 0.5, 1.5)
    light_shift = set_ends(jax.random.randint(keys[3], (LIGHTS,), -1, 2), jax.random.fold_in(keys[3], 1), -1, 1).astype(jnp.int32)
    view_flip = set_ends((jax.random.randint(keys[4], (NX,), 0, 2) < 1).astype(jnp.int32), jax.random.fold_in(keys[4], 1), 0, 1)
    return {"density": density, "albedo": albedo, "light_color": light_color, "light_shift": light_shift, "view_flip": view_flip}


LIGHT_DEPTH = 1.5
VIEW_DEPTH = 2.0


def shift_cells(planes, lateral):
    columns = planes.shape[-1]
    source = jnp.arange(columns, dtype=jnp.int32) - lateral
    inside = (source >= 0) & (source < columns)
    clipped = jnp.broadcast_to(jnp.clip(source, 0, columns - 1), planes.shape)
    picked = jnp.take_along_axis(planes, clipped, axis=-1)
    return jnp.where(inside, picked, jnp.ones_like(picked))


def reference(density, albedo, light_color, light_shift, view_flip):
    rows_total, cells, columns = density.shape
    light_step = LIGHT_DEPTH / rows_total
    view_step = VIEW_DEPTH / cells
    images = []
    for light_id in range(LIGHTS):
        lateral = light_shift[light_id]
        light_tint = light_color[light_id].astype(jnp.float32)

        def march_step(transmit, row_index):
            density_row = density[row_index]
            reflect = albedo[:, row_index].astype(jnp.float32)
            depth_view = density_row * view_step
            running = jnp.cumsum(depth_view, axis=0)
            column_total = running[-1]
            ahead_depth = jnp.where(view_flip[row_index] == 1, column_total[None, :] - running, running - depth_view)
            weights = jnp.exp(-ahead_depth) * (1.0 - jnp.exp(-depth_view))
            colour = jnp.sum(reflect * (weights * transmit)[None], axis=1) * light_tint[:, None]
            opacity = 1.0 - jnp.exp(-column_total)
            image_row = jnp.concatenate([colour, opacity[None]], axis=0)
            return shift_cells(transmit * jnp.exp(-density_row * light_step), lateral), image_row

        _, image_rows = lax.scan(march_step, jnp.ones((cells, columns), jnp.float32), jnp.arange(rows_total, dtype=jnp.int32))
        images.append(jnp.transpose(image_rows, (1, 0, 2)).reshape(4, rows_total * columns))
    return jnp.stack(images)
```

```python
import functools
import jax
import jax.numpy as jnp
from jax import lax
from jax.experimental import pallas as pl
from jax.experimental.pallas import tpu as pltpu
from jax.sharding import PartitionSpec as P

LIGHT_DEPTH = 1.5
VIEW_DEPTH = 2.0
LANES = 128
SUB = 8
SHIFTS = (-1, 0, 1)
MESH = pl.DeviceIdType.MESH


def chunked(plane):
    return jnp.stack([plane[:, k : k + LANES] for k in range(0, plane.shape[1], LANES)])


def slide(planes, amount, fill):
    if amount == 0:
        return planes
    count = planes.shape[0]
    whole, part = divmod(abs(amount), LANES)
    whole = min(whole, count)
    lane = lax.broadcasted_iota(jnp.int32, planes.shape, 2)

    def blocks(n):
        return [jnp.full((n,) + planes.shape[1:], fill, planes.dtype)] if n else []

    if amount > 0:
        if whole:
            planes = jnp.concatenate(blocks(whole) + [planes[: count - whole]] * (whole < count), axis=0)
        if part:
            turned = pltpu.roll(planes, part, 2)
            before = jnp.concatenate(blocks(1) + [turned[:-1]], axis=0)
            planes = jnp.where(lane < part, before, turned)
    else:
        if whole:
            planes = jnp.concatenate([planes[whole:]] * (whole < count) + blocks(whole), axis=0)
        if part:
            turned = pltpu.roll(planes, LANES - part, 2)
            after = jnp.concatenate([turned[1:]] + blocks(1), axis=0)
            planes = jnp.where(lane >= LANES - part, after, turned)
    return planes


def column_sums(planes):
    for bit in (1, 2, 4):
        pairs = planes.reshape(planes.shape[0] // 2, 2, SUB, LANES)
        even, odd = pairs[:, 0], pairs[:, 1]
        row = lax.broadcasted_iota(jnp.int32, even.shape, 1)
        first = (row & bit) == 0
        planes = jnp.where(first, even, odd) + pltpu.roll(jnp.where(first, odd, even), SUB - bit, 1)
    return planes.reshape(planes.shape[0] * SUB, LANES)


def kernel(
    light_count, view_count, density_ref, albedo_ref, flip_ref, out_ref,
    ext, lit, exits, slots, part, part_total, swap, swap_total, comb, comb_total, got, got_total, rows4,
    exit_send, exit_recv, core_send, core_recv, z_send, z_recv,
):
    slices, cells, columns = density_ref.shape
    z_count = view_count // 2
    chunks = columns // LANES
    rows = got.shape[3]
    per_slice = chunks // rows
    light_step = LIGHT_DEPTH / (slices * light_count)
    view_step = VIEW_DEPTH / (cells * view_count)
    me_light = lax.axis_index("light")
    me_view = lax.axis_index("view")
    core = lax.rem(me_view, 2)
    z = lax.div(me_view, 2)
    other = 1 - core

    barrier = pltpu.get_barrier_semaphore()
    for step in range(1, light_count):
        pl.semaphore_signal(barrier, inc=1, device_id=(lax.rem(me_light + step, light_count), me_view), device_id_type=MESH)
    pl.semaphore_signal(barrier, inc=1, device_id=(me_light, z * 2 + other), device_id_type=MESH)
    for step in range(1, z_count):
        pl.semaphore_signal(barrier, inc=1, device_id=(me_light, lax.rem(z + step, z_count) * 2 + core), device_id_type=MESH)

    def fade(x, carry):
        ext[x] = jnp.exp(-chunked(density_ref[x]) * light_step)
        return carry

    lax.fori_loop(0, slices, fade, 0)
    for a, amount in enumerate(SHIFTS):
        exits[a] = lax.fori_loop(
            0, slices, lambda x, e: slide(e * ext[x], amount, 1.0), jnp.ones(ext.shape[1:], jnp.float32)
        )
    for hop in range(light_count - 1):

        @pl.when(hop >= me_light)
        def _():
            for a in range(3):
                slots[a, hop] = jnp.ones(slots.shape[2:], jnp.float32)

    pl.semaphore_wait(barrier, light_count - 1 + 1 + z_count - 1)

    def exit_copy(a, hop):
        return pltpu.make_async_remote_copy(
            src_ref=exits.at[a], dst_ref=slots.at[a, hop],
            send_sem=exit_send.at[a, hop], recv_sem=exit_recv.at[a, hop],
            device_id=(lax.rem(me_light + hop + 1, light_count), me_view), device_id_type=MESH,
        )

    for a in range(3):
        for hop in range(light_count - 1):

            @pl.when(me_light + hop + 1 < light_count)
            def _():
                exit_copy(a, hop).start()

    cell = lax.broadcasted_iota(jnp.int32, (chunks, cells, LANES), 1)

    def weigh(x, carry):
        depth = chunked(density_ref[x]) * view_step
        running = depth
        for step in (1, 2, 4):
            running = running + jnp.where(cell >= step, pltpu.roll(running, step, 1), 0.0)
        suffix = depth
        for step in (1, 2, 4):
            suffix = suffix + jnp.where(cell < cells - step, pltpu.roll(suffix, cells - step, 1), 0.0)
        ahead = jnp.where(flip_ref[x] == 1, suffix, running) - depth
        weight = jnp.exp(-ahead) * (1.0 - jnp.exp(-depth))
        for c in range(3):
            lit[c, x] = weight * chunked(albedo_ref[c, x].astype(jnp.float32))
        total = column_sums(depth)
        for j in range(per_slice):
            piece = x * per_slice + j
            part_total[lax.rem(piece, 2), lax.div(piece, 2)] = total[j * rows : (j + 1) * rows]
        return carry

    lax.fori_loop(0, slices, weigh, 0)

    def core_copy(src, dst, index):
        return pltpu.make_async_remote_copy(
            src_ref=src, dst_ref=dst, send_sem=core_send.at[index], recv_sem=core_recv.at[index],
            device_id=(me_light, z * 2 + other), device_id_type=MESH,
        )

    total_swap = core_copy(part_total.at[other], swap_total, 3)
    total_swap.start()

    def z_copy(src, dst, index, step):
        return pltpu.make_async_remote_copy(
            src_ref=src, dst_ref=dst, send_sem=z_send.at[index, step], recv_sem=z_recv.at[index, z],
            device_id=(me_light, lax.rem(z + step, z_count) * 2 + core), device_id_type=MESH,
        )

    def z_wait(dst, index, step):
        source = lax.rem(z + step, z_count)
        pltpu.make_async_remote_copy(
            src_ref=dst.at[source], dst_ref=dst.at[source], send_sem=z_send.at[index, step],
            recv_sem=z_recv.at[index, source], device_id=(me_light, source * 2 + core), device_id_type=MESH,
        ).wait_recv()

    def flip_of(piece):
        return flip_ref[lax.div(piece, per_slice)]

    total_swap.wait_recv()
    comb_total[...] = part_total[core] + swap_total[...]
    sends = []
    for step in range(1, z_count):
        copy = z_copy(comb_total.at[lax.rem(z + step, z_count)], got_total.at[z], 3, step)
        copy.start()
        sends.append(copy)
    got_total[z] = comb_total[z]

    def enter(a, amount):
        for hop in range(light_count - 1):

            @pl.when(hop < me_light)
            def _():
                exit_copy(a, hop).wait_recv()

        entering = slots[a, light_count - 2]
        for hop in range(light_count - 3, -1, -1):
            entering = slide(entering, amount * slices, 1.0) * slots[a, hop]
        return entering

    def march(a, amount):
        def one(x, trans):
            for c in range(3):
                sums = column_sums(trans * lit[c, x])
                for j in range(per_slice):
                    piece = x * per_slice + j
                    part[a, lax.rem(piece, 2), lax.div(piece, 2), c] = sums[j * rows : (j + 1) * rows]
            return slide(trans * ext[x], amount, 1.0)

        lax.fori_loop(0, slices, one, enter(a, amount))

    def join(a):
        def one(target, carry):
            flip = flip_of(target * 2 + core)
            mine_first = flip == core
            mine_fade = jnp.where(mine_first, 1.0, jnp.exp(-swap_total[target]))
            their_fade = jnp.where(mine_first, jnp.exp(-part_total[core, target]), 1.0)
            for c in range(3):
                comb[a, target, c] = mine_fade * part[a, core, target, c] + their_fade * swap[a, target, c]
            return carry

        lax.fori_loop(0, z_count, one, 0)

    swaps = []

    def finish_swap(a):
        swaps[a].wait_recv()
        join(a)
        for step in range(1, z_count):
            copy = z_copy(comb.at[a, lax.rem(z + step, z_count)], got.at[a, z], a, step)
            copy.start()
            sends.append(copy)
        got[a, z] = comb[a, z]

    for a, amount in enumerate(SHIFTS):
        march(a, amount)
        copy = core_copy(part.at[a, other], swap.at[a], a)
        copy.start()
        swaps.append(copy)
        if a > 0:
            finish_swap(a - 1)
    finish_swap(2)

    for step in range(1, z_count):
        z_wait(got_total, 3, step)
    flip = flip_of(me_view)
    before = jnp.zeros(got_total.shape[1:], jnp.float32)
    fades = []
    for source in range(z_count):
        fades.append(before)
        before = before + got_total[source]
    for source in range(z_count):
        depth = jnp.where(flip == 1, before - fades[source] - got_total[source], fades[source])
        fades[source] = jnp.exp(-depth)
    opacity = 1.0 - jnp.exp(-before)
    for a in range(3):
        for step in range(1, z_count):
            z_wait(got.at[a], a, step)
        for c in range(3):
            value = fades[0] * got[a, 0, c]
            for source in range(1, z_count):
                value = value + fades[source] * got[a, source, c]
            rows4[a, pl.ds(c, rows, stride=4), :] = value
        rows4[a, pl.ds(3, rows, stride=4), :] = opacity
        for r in range(rows):
            out_ref[a, :, r * LANES : (r + 1) * LANES] = rows4[a, r * 4 : (r + 1) * 4, :]

    for copy in sends:
        copy.wait_send()
    for copy in swaps:
        copy.wait_send()
    total_swap.wait_send()
    for a in range(3):
        for hop in range(light_count - 1):

            @pl.when(me_light + hop + 1 < light_count)
            def _():
                exit_copy(a, hop).wait_send()


def local(density, albedo, light_color, light_shift, view_flip):
    slices, cells, columns = density.shape
    light_count = lax.axis_size("light")
    view_count = lax.axis_size("view")
    z_count = view_count // 2
    chunks = columns // LANES
    piece = slices * columns // view_count
    rows = piece // LANES
    f32 = jnp.float32
    vmem = pl.BlockSpec(memory_space=pltpu.VMEM)
    dma = pltpu.SemaphoreType.DMA
    planes = pl.pallas_call(
        functools.partial(kernel, light_count, view_count),
        out_shape=jax.ShapeDtypeStruct((3, 4, piece), f32),
        in_specs=[vmem, vmem, pl.BlockSpec(memory_space=pltpu.SMEM)],
        out_specs=vmem,
        scratch_shapes=[
            pltpu.VMEM((slices, chunks, cells, LANES), f32),
            pltpu.VMEM((3, slices, chunks, cells, LANES), f32),
            pltpu.VMEM((3, chunks, cells, LANES), f32),
            pltpu.VMEM((3, light_count - 1, chunks, cells, LANES), f32),
            pltpu.VMEM((3, 2, z_count, 3, rows, LANES), f32),
            pltpu.VMEM((2, z_count, rows, LANES), f32),
            pltpu.VMEM((3, z_count, 3, rows, LANES), f32),
            pltpu.VMEM((z_count, rows, LANES), f32),
            pltpu.VMEM((3, z_count, 3, rows, LANES), f32),
            pltpu.VMEM((z_count, rows, LANES), f32),
            pltpu.VMEM((3, z_count, 3, rows, LANES), f32),
            pltpu.VMEM((z_count, rows, LANES), f32),
            pltpu.VMEM((3, rows * 4, LANES), f32),
            dma((3, light_count - 1)),
            dma((3, light_count - 1)),
            dma((4,)),
            dma((4,)),
            dma((4, z_count)),
            dma((4, z_count)),
        ],
        compiler_params=pltpu.CompilerParams(
            collective_id=0, has_side_effects=True, vmem_limit_bytes=32 * 2**20
        ),
    )(density, albedo, view_flip)
    lateral = light_shift[:, None, None]
    picked = jnp.where(lateral == 1, planes[2][None], jnp.where(lateral == -1, planes[0][None], planes[1][None]))
    tint = jnp.concatenate([light_color, jnp.ones((light_color.shape[0], 1), f32)], axis=1)
    return picked * tint[:, :, None]


def solution(mesh):
    return jax.shard_map(
        local,
        mesh=mesh,
        in_specs=(P("light", "view", None), P(None, "light", "view", None), P(), P(), P("light")),
        out_specs=P(None, None, ("light", "view")),
        check_vma=False,
    )
```

```python
import functools
import jax
import jax.numpy as jnp
from jax import lax
from jax.experimental import pallas as pl
from jax.experimental.pallas import tpu as pltpu
from jax.sharding import PartitionSpec as P

LIGHT_DEPTH = 1.5
VIEW_DEPTH = 2.0
LANES = 128
SUB = 8
SHIFTS = (-1, 0, 1)
MESH = pl.DeviceIdType.MESH


def chunked(plane):
    return jnp.stack([plane[:, k : k + LANES] for k in range(0, plane.shape[1], LANES)])


def slide(planes, amount, fill):
    if amount == 0:
        return planes
    count = planes.shape[0]
    whole, part = divmod(abs(amount), LANES)
    whole = min(whole, count)
    lane = lax.broadcasted_iota(jnp.int32, planes.shape, 2)

    def blocks(n):
        return [jnp.full((n,) + planes.shape[1:], fill, planes.dtype)] if n else []

    if amount > 0:
        if whole:
            planes = jnp.concatenate(blocks(whole) + [planes[: count - whole]] * (whole < count), axis=0)
        if part:
            turned = pltpu.roll(planes, part, 2)
            before = jnp.concatenate(blocks(1) + [turned[:-1]], axis=0)
            planes = jnp.where(lane < part, before, turned)
    else:
        if whole:
            planes = jnp.concatenate([planes[whole:]] * (whole < count) + blocks(whole), axis=0)
        if part:
            turned = pltpu.roll(planes, LANES - part, 2)
            after = jnp.concatenate([turned[1:]] + blocks(1), axis=0)
            planes = jnp.where(lane >= LANES - part, after, turned)
    return planes


def column_sums(planes):
    for bit in (1, 2, 4):
        pairs = planes.reshape(planes.shape[0] // 2, 2, SUB, LANES)
        even, odd = pairs[:, 0], pairs[:, 1]
        row = lax.broadcasted_iota(jnp.int32, even.shape, 1)
        first = (row & bit) == 0
        planes = jnp.where(first, even, odd) + pltpu.roll(jnp.where(first, odd, even), SUB - bit, 1)
    return planes.reshape(planes.shape[0] * SUB, LANES)


def kernel(
    light_count, view_count, density_hbm, albedo_hbm, color_hbm, shift_hbm, flip_hbm, out_ref,
    density, albedo, color, lateral, flips, ahead_of, tinted, totals, entered, received,
    part, part_total, swap, swap_total, comb, comb_total, got, got_total, rows4,
    load_sem, exit_send, exit_recv, core_send, core_recv, z_send, z_recv,
):
    slices, cells, columns = density.shape
    lights = color.shape[1]
    z_count = view_count // 2
    stages = light_count.bit_length() - 1
    chunks = columns // LANES
    rows = got.shape[3]
    per_slice = chunks // rows
    light_step = LIGHT_DEPTH / (slices * light_count)
    view_step = VIEW_DEPTH / (cells * view_count)

    loads = [
        pltpu.make_async_copy(density_hbm.at[x], density.at[x], load_sem.at[x]) for x in range(slices)
    ] + [
        pltpu.make_async_copy(src, dst, load_sem.at[slices + i])
        for i, (src, dst) in enumerate(
            ((flip_hbm, flips), (albedo_hbm, albedo), (shift_hbm, lateral), (color_hbm, color))
        )
    ]
    for load in loads:
        load.start()

    me_light = lax.axis_index("light")
    me_view = lax.axis_index("view")
    core = lax.rem(me_view, 2)
    z = lax.div(me_view, 2)
    other = 1 - core

    def partner(b):
        bit = lax.rem(lax.div(me_light, 2**b), 2)
        return me_light + (1 - 2 * bit) * 2**b

    barrier = pltpu.get_barrier_semaphore()
    for b in range(stages):
        pl.semaphore_signal(barrier, inc=1, device_id=(partner(b), me_view), device_id_type=MESH)
    pl.semaphore_signal(barrier, inc=1, device_id=(me_light, z * 2 + other), device_id_type=MESH)
    for step in range(1, z_count):
        pl.semaphore_signal(barrier, inc=1, device_id=(me_light, lax.rem(z + step, z_count) * 2 + core), device_id_type=MESH)

    ones = jnp.ones((chunks, cells, LANES), jnp.float32)
    chain = [ones] * 3
    for x in range(slices):
        loads[x].wait()
        ext = jnp.exp(-chunked(density[x]) * light_step)
        for a, amount in enumerate(SHIFTS):
            ahead_of[a, x] = chain[a]
            chain[a] = slide(chain[a] * ext, amount, 1.0)
    for a in range(3):
        totals[a, 0] = chain[a]
        entered[a] = ones

    pl.semaphore_wait(barrier, stages + 1 + z_count - 1)

    def facts(b):
        bit = lax.rem(lax.div(me_light, 2**b), 2)
        upward = lax.div(me_light, 2 ** (b + 1)) != light_count // 2 ** (b + 1) - 1
        return bit, upward

    def exit_copy(a, b):
        return pltpu.make_async_remote_copy(
            src_ref=totals.at[a, b], dst_ref=received.at[a, b],
            send_sem=exit_send.at[a, b], recv_sem=exit_recv.at[a, b],
            device_id=(partner(b), me_view), device_id_type=MESH,
        )

    def send_exit(a, b):
        bit, upward = facts(b)

        @pl.when((bit == 0) | upward)
        def _():
            exit_copy(a, b).start()

    def advance(a, b):
        amount = SHIFTS[a]
        bit, upward = facts(b)

        @pl.when((bit == 1) | upward)
        def _():
            exit_copy(a, b).wait_recv()

        @pl.when(bit == 1)
        def _():
            moved = received[a, b]
            for k in range(b):
                inner = lax.rem(lax.div(me_light, 2**k), 2)
                moved = jnp.where(inner == 1, slide(moved, amount * slices * 2**k, 1.0), moved)
            entered[a] = moved * entered[a]

        if b + 1 < stages:

            @pl.when(upward)
            def _():
                mine, theirs = totals[a, b], received[a, b]
                lower = jnp.where(bit == 1, theirs, mine)
                upper = jnp.where(bit == 1, mine, theirs)
                totals[a, b + 1] = slide(lower, amount * slices * 2**b, 1.0) * upper

            send_exit(a, b + 1)

    for a in range(3):
        send_exit(a, 0)

    loads[slices].wait()
    loads[slices + 1].wait()
    cell = lax.broadcasted_iota(jnp.int32, (chunks, cells, LANES), 1)
    for x in range(slices):
        depth = chunked(density[x]) * view_step
        running = depth
        for step in (1, 2, 4):
            running = running + jnp.where(cell >= step, pltpu.roll(running, step, 1), 0.0)
        column = jnp.broadcast_to(running[:, cells - 1 :, :], running.shape)
        ahead = jnp.where(flips[x] == 1, column - running, running - depth)
        weight = jnp.exp(-ahead) * (1.0 - jnp.exp(-depth))
        for c in range(3):
            tinted[c, x] = weight * chunked(albedo[c, x].astype(jnp.float32))
        total = column_sums(depth)
        for j in range(per_slice):
            piece = x * per_slice + j
            part_total[piece % 2, piece // 2] = total[j * rows : (j + 1) * rows]

    def core_copy(src, dst, index):
        return pltpu.make_async_remote_copy(
            src_ref=src, dst_ref=dst, send_sem=core_send.at[index], recv_sem=core_recv.at[index],
            device_id=(me_light, z * 2 + other), device_id_type=MESH,
        )

    total_swap = core_copy(part_total.at[other], swap_total, 3)
    total_swap.start()

    def z_copy(src, dst, index, step):
        return pltpu.make_async_remote_copy(
            src_ref=src, dst_ref=dst, send_sem=z_send.at[index, step], recv_sem=z_recv.at[index, z],
            device_id=(me_light, lax.rem(z + step, z_count) * 2 + core), device_id_type=MESH,
        )

    def z_wait(dst, index, step):
        source = lax.rem(z + step, z_count)
        pltpu.make_async_remote_copy(
            src_ref=dst.at[source], dst_ref=dst.at[source], send_sem=z_send.at[index, step],
            recv_sem=z_recv.at[index, source], device_id=(me_light, source * 2 + core), device_id_type=MESH,
        ).wait_recv()

    def flip_of(piece):
        return flips[lax.div(piece, per_slice)]

    sends = []
    swaps = []

    def share_totals():
        total_swap.wait_recv()
        comb_total[...] = part_total[core] + swap_total[...]
        for step in range(1, z_count):
            copy = z_copy(comb_total.at[lax.rem(z + step, z_count)], got_total.at[z], 3, step)
            copy.start()
            sends.append(copy)
        got_total[z] = comb_total[z]
        for target in range(z_count):
            mine_first = flip_of(target * 2 + core) == core
            mine, theirs = part_total[core, target], swap_total[target]
            part_total[core, target] = jnp.where(mine_first, 1.0, jnp.exp(-theirs))
            swap_total[target] = jnp.where(mine_first, jnp.exp(-mine), 1.0)

    def march(a):
        entering = entered[a]
        for x in range(slices):
            trans = slide(entering, SHIFTS[a] * x, 1.0) * ahead_of[a, x]
            for c in range(3):
                sums = column_sums(trans * tinted[c, x])
                for j in range(per_slice):
                    piece = x * per_slice + j
                    part[a, piece % 2, piece // 2, c] = sums[j * rows : (j + 1) * rows]
        copy = core_copy(part.at[a, other], swap.at[a], a)
        copy.start()
        swaps.append(copy)

    def finish_swap(a):
        swaps[a].wait_recv()
        for target in range(z_count):
            mine_fade, their_fade = part_total[core, target], swap_total[target]
            for c in range(3):
                comb[a, target, c] = mine_fade * part[a, core, target, c] + their_fade * swap[a, target, c]
        for step in range(1, z_count):
            copy = z_copy(comb.at[a, lax.rem(z + step, z_count)], got.at[a, z], a, step)
            copy.start()
            sends.append(copy)
        got[a, z] = comb[a, z]

    for wave in range(stages + 2):
        for a in range(2, -1, -1):
            b = wave - a
            if 0 <= b < stages:
                advance(a, b)
            if wave == 0 and a == 0:
                share_totals()
            if b == stages - 1:
                march(a)
                if a > 0:
                    finish_swap(a - 1)
    finish_swap(2)

    loads[slices + 2].wait()
    loads[slices + 3].wait()
    for step in range(1, z_count):
        z_wait(got_total, 3, step)
    flip = flip_of(me_view)
    before = jnp.zeros(got_total.shape[1:], jnp.float32)
    fades = []
    for source in range(z_count):
        fades.append(before)
        before = before + got_total[source]
    for source in range(z_count):
        depth = jnp.where(flip == 1, before - fades[source] - got_total[source], fades[source])
        fades[source] = jnp.exp(-depth)
    opacity = 1.0 - jnp.exp(-before)
    for a in range(3):
        for step in range(1, z_count):
            z_wait(got.at[a], a, step)
        for c in range(3):
            value = fades[0] * got[a, 0, c]
            for source in range(1, z_count):
                value = value + fades[source] * got[a, source, c]
            rows4[a, pl.ds(c, rows, stride=4), :] = value
        rows4[a, pl.ds(3, rows, stride=4), :] = opacity
    field = lax.rem(lax.broadcasted_iota(jnp.int32, rows4.shape[1:], 0), 4)
    for light in range(lights):
        step = lateral[light]
        picked = jnp.where(step == SHIFTS[2], rows4[2], jnp.where(step == SHIFTS[0], rows4[0], rows4[1]))
        tint = jnp.where(
            field == 0, color[0, light], jnp.where(field == 1, color[1, light], jnp.where(field == 2, color[2, light], 1.0))
        )
        lit = picked * tint
        for r in range(rows):
            out_ref[light, :, r * LANES : (r + 1) * LANES] = lit[r * 4 : (r + 1) * 4, :]

    for copy in sends:
        copy.wait_send()
    for copy in swaps:
        copy.wait_send()
    total_swap.wait_send()
    for b in range(stages):
        bit, upward = facts(b)

        @pl.when((bit == 0) | upward)
        def _():
            for a in range(3):
                exit_copy(a, b).wait_send()


def local(density, albedo, light_color, light_shift, view_flip):
    slices, cells, columns = density.shape
    lights = light_shift.shape[0]
    light_count = lax.axis_size("light")
    view_count = lax.axis_size("view")
    z_count = view_count // 2
    stages = light_count.bit_length() - 1
    chunks = columns // LANES
    piece = slices * columns // view_count
    rows = piece // LANES
    f32 = jnp.float32
    anywhere = pl.BlockSpec(memory_space=pl.ANY)
    dma = pltpu.SemaphoreType.DMA
    return pl.pallas_call(
        functools.partial(kernel, light_count, view_count),
        out_shape=jax.ShapeDtypeStruct((lights, 4, piece), f32),
        in_specs=[anywhere] * 5,
        out_specs=pl.BlockSpec(memory_space=pltpu.VMEM),
        scratch_shapes=[
            pltpu.VMEM(density.shape, f32),
            pltpu.VMEM(albedo.shape, albedo.dtype),
            pltpu.SMEM((3, lights), f32),
            pltpu.SMEM((lights,), jnp.int32),
            pltpu.SMEM((slices,), jnp.int32),
            pltpu.VMEM((3, slices, chunks, cells, LANES), f32),
            pltpu.VMEM((3, slices, chunks, cells, LANES), f32),
            pltpu.VMEM((3, stages, chunks, cells, LANES), f32),
            pltpu.VMEM((3, chunks, cells, LANES), f32),
            pltpu.VMEM((3, stages, chunks, cells, LANES), f32),
            pltpu.VMEM((3, 2, z_count, 3, rows, LANES), f32),
            pltpu.VMEM((2, z_count, rows, LANES), f32),
            pltpu.VMEM((3, z_count, 3, rows, LANES), f32),
            pltpu.VMEM((z_count, rows, LANES), f32),
            pltpu.VMEM((3, z_count, 3, rows, LANES), f32),
            pltpu.VMEM((z_count, rows, LANES), f32),
            pltpu.VMEM((3, z_count, 3, rows, LANES), f32),
            pltpu.VMEM((z_count, rows, LANES), f32),
            pltpu.VMEM((3, rows * 4, LANES), f32),
            dma((slices + 4,)),
            dma((3, stages)),
            dma((3, stages)),
            dma((4,)),
            dma((4,)),
            dma((4, z_count)),
            dma((4, z_count)),
        ],
        compiler_params=pltpu.CompilerParams(
            collective_id=0, has_side_effects=True, vmem_limit_bytes=56 * 2**20
        ),
    )(density, albedo, light_color.T, light_shift, view_flip)


def solution(mesh):
    return jax.shard_map(
        local,
        mesh=mesh,
        in_specs=(P("light", "view", None), P(None, "light", "view", None), P(), P(), P("light")),
        out_specs=P(None, None, ("light", "view")),
        check_vma=False,
    )
```

```python
import functools
import jax
import jax.numpy as jnp
from jax import lax
from jax.experimental import pallas as pl
from jax.experimental.pallas import tpu as pltpu
from jax.sharding import PartitionSpec as P

LIGHT_DEPTH = 1.5
VIEW_DEPTH = 2.0
LANES = 128
SUB = 8
SHIFTS = (-1, 0, 1)
MESH = pl.DeviceIdType.MESH


def chunked(plane):
    return jnp.stack([plane[:, k : k + LANES] for k in range(0, plane.shape[1], LANES)])


def slide(planes, amount, fill):
    if amount == 0:
        return planes
    count = planes.shape[0]
    whole, part = divmod(abs(amount), LANES)
    whole = min(whole, count)
    lane = lax.broadcasted_iota(jnp.int32, planes.shape, 2)

    def blocks(n):
        return [jnp.full((n,) + planes.shape[1:], fill, planes.dtype)] if n else []

    if amount > 0:
        if whole:
            planes = jnp.concatenate(blocks(whole) + [planes[: count - whole]] * (whole < count), axis=0)
        if part:
            turned = pltpu.roll(planes, part, 2)
            before = jnp.concatenate(blocks(1) + [turned[:-1]], axis=0)
            planes = jnp.where(lane < part, before, turned)
    else:
        if whole:
            planes = jnp.concatenate([planes[whole:]] * (whole < count) + blocks(whole), axis=0)
        if part:
            turned = pltpu.roll(planes, LANES - part, 2)
            after = jnp.concatenate([turned[1:]] + blocks(1), axis=0)
            planes = jnp.where(lane >= LANES - part, after, turned)
    return planes


def column_sums(planes):
    for bit in (1, 2, 4):
        pairs = planes.reshape(planes.shape[0] // 2, 2, SUB, LANES)
        even, odd = pairs[:, 0], pairs[:, 1]
        row = lax.broadcasted_iota(jnp.int32, even.shape, 1)
        first = (row & bit) == 0
        planes = jnp.where(first, even, odd) + pltpu.roll(jnp.where(first, odd, even), SUB - bit, 1)
    return planes.reshape(planes.shape[0] * SUB, LANES)


def kernel(
    light_count, view_count, density_hbm, albedo_hbm, color_hbm, shift_hbm, flip_hbm,
    out0, out1, out2, tint0, tint1, tint2,
    density, albedo, color, lateral, flips, ahead_of, tinted, totals, entered, received,
    part, part_total, swap, swap_total, comb, comb_total, got, got_total, rows4, planes, tints,
    load_sem, store_sem, exit_send, exit_recv, core_send, core_recv, z_send, z_recv,
):
    slices, cells, columns = density.shape
    lights = color.shape[1]
    z_count = view_count // 2
    stages = light_count.bit_length() - 1
    chunks = columns // LANES
    rows = got.shape[3]
    per_slice = chunks // rows
    light_step = LIGHT_DEPTH / (slices * light_count)
    view_step = VIEW_DEPTH / (cells * view_count)

    loads = [
        pltpu.make_async_copy(density_hbm.at[x], density.at[x], load_sem.at[x]) for x in range(slices)
    ] + [
        pltpu.make_async_copy(src, dst, load_sem.at[slices + i])
        for i, (src, dst) in enumerate(
            ((flip_hbm, flips), (albedo_hbm, albedo), (shift_hbm, lateral), (color_hbm, color))
        )
    ]
    for load in loads:
        load.start()

    me_light = lax.axis_index("light")
    me_view = lax.axis_index("view")
    core = lax.rem(me_view, 2)
    z = lax.div(me_view, 2)
    other = 1 - core

    def partner(b):
        bit = lax.rem(lax.div(me_light, 2**b), 2)
        return me_light + (1 - 2 * bit) * 2**b

    barrier = pltpu.get_barrier_semaphore()
    for b in range(stages):
        pl.semaphore_signal(barrier, inc=1, device_id=(partner(b), me_view), device_id_type=MESH)
    pl.semaphore_signal(barrier, inc=1, device_id=(me_light, z * 2 + other), device_id_type=MESH)
    for step in range(1, z_count):
        pl.semaphore_signal(barrier, inc=1, device_id=(me_light, lax.rem(z + step, z_count) * 2 + core), device_id_type=MESH)

    ones = jnp.ones((chunks, cells, LANES), jnp.float32)
    chain = [ones] * 3
    for x in range(slices):
        loads[x].wait()
        ext = jnp.exp(-chunked(density[x]) * light_step)
        for a, amount in enumerate(SHIFTS):
            ahead_of[a, x] = chain[a]
            chain[a] = slide(chain[a] * ext, amount, 1.0)
    for a in range(3):
        totals[a, 0] = chain[a]
        entered[a] = ones

    pl.semaphore_wait(barrier, stages + 1 + z_count - 1)

    def facts(b):
        bit = lax.rem(lax.div(me_light, 2**b), 2)
        upward = lax.div(me_light, 2 ** (b + 1)) != light_count // 2 ** (b + 1) - 1
        return bit, upward

    def exit_copy(a, b):
        return pltpu.make_async_remote_copy(
            src_ref=totals.at[a, b], dst_ref=received.at[a, b],
            send_sem=exit_send.at[a, b], recv_sem=exit_recv.at[a, b],
            device_id=(partner(b), me_view), device_id_type=MESH,
        )

    def send_exit(a, b):
        bit, upward = facts(b)

        @pl.when((bit == 0) | upward)
        def _():
            exit_copy(a, b).start()

    def advance(a, b):
        amount = SHIFTS[a]
        bit, upward = facts(b)

        @pl.when((bit == 1) | upward)
        def _():
            exit_copy(a, b).wait_recv()

        @pl.when(bit == 1)
        def _():
            moved = received[a, b]
            for k in range(b):
                inner = lax.rem(lax.div(me_light, 2**k), 2)
                moved = jnp.where(inner == 1, slide(moved, amount * slices * 2**k, 1.0), moved)
            entered[a] = moved * entered[a]

        if b + 1 < stages:

            @pl.when(upward)
            def _():
                mine, theirs = totals[a, b], received[a, b]
                lower = jnp.where(bit == 1, theirs, mine)
                upper = jnp.where(bit == 1, mine, theirs)
                totals[a, b + 1] = slide(lower, amount * slices * 2**b, 1.0) * upper

            send_exit(a, b + 1)

    def drain_exit(a):
        bit, upward = facts(0)

        @pl.when((bit == 0) | upward)
        def _():
            exit_copy(a, 0).wait_send()

    send_exit(0, 0)
    loads[slices].wait()
    loads[slices + 1].wait()
    cell = lax.broadcasted_iota(jnp.int32, (chunks, cells, LANES), 1)
    for x in range(slices):
        depth = chunked(density[x]) * view_step
        running = depth
        for step in (1, 2, 4):
            running = running + jnp.where(cell >= step, pltpu.roll(running, step, 1), 0.0)
        column = jnp.broadcast_to(running[:, cells - 1 :, :], running.shape)
        ahead = jnp.where(flips[x] == 1, column - running, running - depth)
        weight = jnp.exp(-ahead) * (1.0 - jnp.exp(-depth))
        for c in range(3):
            tinted[c, x] = weight * chunked(albedo[c, x].astype(jnp.float32))
        total = column_sums(depth)
        for j in range(per_slice):
            piece = x * per_slice + j
            part_total[piece % 2, piece // 2] = total[j * rows : (j + 1) * rows]
        for a in (1, 2):
            if x + 1 == a * slices // 3:
                drain_exit(a - 1)
                send_exit(a, 0)

    def core_copy(src, dst, index):
        return pltpu.make_async_remote_copy(
            src_ref=src, dst_ref=dst, send_sem=core_send.at[index], recv_sem=core_recv.at[index],
            device_id=(me_light, z * 2 + other), device_id_type=MESH,
        )

    total_swap = core_copy(part_total.at[other], swap_total, 3)
    total_swap.start()

    def z_copy(src, dst, index, step):
        return pltpu.make_async_remote_copy(
            src_ref=src, dst_ref=dst, send_sem=z_send.at[index, step], recv_sem=z_recv.at[index, z],
            device_id=(me_light, lax.rem(z + step, z_count) * 2 + core), device_id_type=MESH,
        )

    def z_wait(dst, index, step):
        source = lax.rem(z + step, z_count)
        pltpu.make_async_remote_copy(
            src_ref=dst.at[source], dst_ref=dst.at[source], send_sem=z_send.at[index, step],
            recv_sem=z_recv.at[index, source], device_id=(me_light, source * 2 + core), device_id_type=MESH,
        ).wait_recv()

    def flip_of(piece):
        return flips[lax.div(piece, per_slice)]

    loads[slices + 2].wait()
    loads[slices + 3].wait()
    lane = lax.broadcasted_iota(jnp.int32, tints.shape[1:], 1)
    for light in range(lights):
        red, green, blue = (color[c, light] for c in range(3))
        tint = jnp.where(lane == 0, red, jnp.where(lane == 1, green, jnp.where(lane == 2, blue, 1.0)))
        step = lateral[light]
        for a, amount in enumerate(SHIFTS):
            tints[a, light : light + 1, :] = jnp.where(step == amount, tint, 0.0)[light : light + 1]
    stores = []
    for a, target in enumerate((tint0, tint1, tint2)):
        store = pltpu.make_async_copy(tints.at[a], target, store_sem.at[3 + a])
        store.start()
        stores.append(store)

    sends = []
    swaps = []

    def share_totals():
        total_swap.wait_recv()
        comb_total[...] = part_total[core] + swap_total[...]
        for step in range(1, z_count):
            copy = z_copy(comb_total.at[lax.rem(z + step, z_count)], got_total.at[z], 3, step)
            copy.start()
            sends.append(copy)
        got_total[z] = comb_total[z]
        for target in range(z_count):
            mine_first = flip_of(target * 2 + core) == core
            mine, theirs = part_total[core, target], swap_total[target]
            part_total[core, target] = jnp.where(mine_first, 1.0, jnp.exp(-theirs))
            swap_total[target] = jnp.where(mine_first, jnp.exp(-mine), 1.0)

    def march(a):
        entering = entered[a]
        for x in range(slices):
            trans = slide(entering, SHIFTS[a] * x, 1.0) * ahead_of[a, x]
            for c in range(3):
                sums = column_sums(trans * tinted[c, x])
                for j in range(per_slice):
                    piece = x * per_slice + j
                    part[a, piece % 2, piece // 2, c] = sums[j * rows : (j + 1) * rows]
        copy = core_copy(part.at[a, other], swap.at[a], a)
        copy.start()
        swaps.append(copy)

    def finish_swap(a):
        swaps[a].wait_recv()
        for target in range(z_count):
            mine_fade, their_fade = part_total[core, target], swap_total[target]
            for c in range(3):
                comb[a, target, c] = mine_fade * part[a, core, target, c] + their_fade * swap[a, target, c]
        for step in range(1, z_count):
            copy = z_copy(comb.at[a, lax.rem(z + step, z_count)], got.at[a, z], a, step)
            copy.start()
            sends.append(copy)
        got[a, z] = comb[a, z]

    for wave in range(stages + 2):
        for a in range(2, -1, -1):
            b = wave - a
            if 0 <= b < stages:
                advance(a, b)
            if wave == 0 and a == 0:
                share_totals()
            if b == stages - 1:
                march(a)
                if a > 0:
                    finish_swap(a - 1)
    finish_swap(2)

    for step in range(1, z_count):
        z_wait(got_total, 3, step)
    flip = flip_of(me_view)
    before = jnp.zeros(got_total.shape[1:], jnp.float32)
    fades = []
    for source in range(z_count):
        fades.append(before)
        before = before + got_total[source]
    for source in range(z_count):
        depth = jnp.where(flip == 1, before - fades[source] - got_total[source], fades[source])
        fades[source] = jnp.exp(-depth)
    opacity = 1.0 - jnp.exp(-before)
    for a in range(3):
        for step in range(1, z_count):
            z_wait(got.at[a], a, step)
        for c in range(3):
            value = fades[0] * got[a, 0, c]
            for source in range(1, z_count):
                value = value + fades[source] * got[a, source, c]
            rows4[a, pl.ds(c, rows, stride=4), :] = value
        rows4[a, pl.ds(3, rows, stride=4), :] = opacity
        for r in range(rows):
            planes[a, :, r * LANES : (r + 1) * LANES] = rows4[a, r * 4 : (r + 1) * 4, :]
        store = pltpu.make_async_copy(planes.at[a], (out0, out1, out2)[a], store_sem.at[a])
        store.start()
        stores.append(store)

    for store in stores:
        store.wait()
    for copy in sends:
        copy.wait_send()
    for copy in swaps:
        copy.wait_send()
    total_swap.wait_send()
    for b in range(stages):
        bit, upward = facts(b)

        @pl.when((bit == 0) | upward)
        def _():
            for a in range(2 if b == 0 else 0, 3):
                exit_copy(a, b).wait_send()


def local(density, albedo, light_color, light_shift, view_flip):
    slices, cells, columns = density.shape
    lights = light_shift.shape[0]
    light_count = lax.axis_size("light")
    view_count = lax.axis_size("view")
    z_count = view_count // 2
    stages = light_count.bit_length() - 1
    chunks = columns // LANES
    piece = slices * columns // view_count
    rows = piece // LANES
    f32 = jnp.float32
    anywhere = pl.BlockSpec(memory_space=pl.ANY)
    dma = pltpu.SemaphoreType.DMA
    outs = pl.pallas_call(
        functools.partial(kernel, light_count, view_count),
        out_shape=(
            *[jax.ShapeDtypeStruct((4, piece), f32)] * 3,
            *[jax.ShapeDtypeStruct((lights, 4), f32)] * 3,
        ),
        in_specs=[anywhere] * 5,
        out_specs=[anywhere] * 6,
        scratch_shapes=[
            pltpu.VMEM(density.shape, f32),
            pltpu.VMEM(albedo.shape, albedo.dtype),
            pltpu.SMEM((3, lights), f32),
            pltpu.SMEM((lights,), jnp.int32),
            pltpu.SMEM((slices,), jnp.int32),
            pltpu.VMEM((3, slices, chunks, cells, LANES), f32),
            pltpu.VMEM((3, slices, chunks, cells, LANES), f32),
            pltpu.VMEM((3, stages, chunks, cells, LANES), f32),
            pltpu.VMEM((3, chunks, cells, LANES), f32),
            pltpu.VMEM((3, stages, chunks, cells, LANES), f32),
            pltpu.VMEM((3, 2, z_count, 3, rows, LANES), f32),
            pltpu.VMEM((2, z_count, rows, LANES), f32),
            pltpu.VMEM((3, z_count, 3, rows, LANES), f32),
            pltpu.VMEM((z_count, rows, LANES), f32),
            pltpu.VMEM((3, z_count, 3, rows, LANES), f32),
            pltpu.VMEM((z_count, rows, LANES), f32),
            pltpu.VMEM((3, z_count, 3, rows, LANES), f32),
            pltpu.VMEM((z_count, rows, LANES), f32),
            pltpu.VMEM((3, rows * 4, LANES), f32),
            pltpu.VMEM((3, 4, piece), f32),
            pltpu.VMEM((3, lights, 4), f32),
            dma((slices + 4,)),
            dma((6,)),
            dma((3, stages)),
            dma((3, stages)),
            dma((4,)),
            dma((4,)),
            dma((4, z_count)),
            dma((4, z_count)),
        ],
        compiler_params=pltpu.CompilerParams(
            collective_id=0, has_side_effects=True, vmem_limit_bytes=56 * 2**20
        ),
    )(density, albedo, light_color.T, light_shift, view_flip)
    planes, tints = outs[:3], outs[3:]
    image = tints[0][:, :, None] * planes[0][None]
    for a in range(1, 3):
        image = image + tints[a][:, :, None] * planes[a][None]
    return image


def solution(mesh):
    return jax.shard_map(
        local,
        mesh=mesh,
        in_specs=(P("light", "view", None), P(None, "light", "view", None), P(), P(), P("light")),
        out_specs=P(None, None, ("light", "view")),
        check_vma=False,
    )
```

```python
import functools
import jax
import jax.numpy as jnp
from jax import lax
from jax.experimental import pallas as pl
from jax.experimental.pallas import tpu as pltpu
from jax.sharding import PartitionSpec as P

LIGHT_DEPTH = 1.5
VIEW_DEPTH = 2.0
LANES = 128
SUB = 8
SHIFTS = (-1, 0, 1)
MESH = pl.DeviceIdType.MESH


def chunked(plane):
    return jnp.stack([plane[:, k : k + LANES] for k in range(0, plane.shape[1], LANES)])


def slide(planes, amount, fill):
    if amount == 0:
        return planes
    count = planes.shape[0]
    whole, part = divmod(abs(amount), LANES)
    whole = min(whole, count)
    lane = lax.broadcasted_iota(jnp.int32, planes.shape, 2)

    def blocks(n):
        return [jnp.full((n,) + planes.shape[1:], fill, planes.dtype)] if n else []

    if amount > 0:
        if whole:
            planes = jnp.concatenate(blocks(whole) + [planes[: count - whole]] * (whole < count), axis=0)
        if part:
            turned = pltpu.roll(planes, part, 2)
            before = jnp.concatenate(blocks(1) + [turned[:-1]], axis=0)
            planes = jnp.where(lane < part, before, turned)
    else:
        if whole:
            planes = jnp.concatenate([planes[whole:]] * (whole < count) + blocks(whole), axis=0)
        if part:
            turned = pltpu.roll(planes, LANES - part, 2)
            after = jnp.concatenate([turned[1:]] + blocks(1), axis=0)
            planes = jnp.where(lane >= LANES - part, after, turned)
    return planes


def column_sums(planes):
    for bit in (1, 2, 4):
        pairs = planes.reshape(planes.shape[0] // 2, 2, SUB, LANES)
        even, odd = pairs[:, 0], pairs[:, 1]
        row = lax.broadcasted_iota(jnp.int32, even.shape, 1)
        first = (row & bit) == 0
        planes = jnp.where(first, even, odd) + pltpu.roll(jnp.where(first, odd, even), SUB - bit, 1)
    return planes.reshape(planes.shape[0] * SUB, LANES)


def kernel(
    light_count, view_count, density_hbm, albedo_hbm, color_hbm, shift_hbm, flip_hbm, out_ref,
    density, albedo, color, lateral, flips, ahead_of, tinted, totals, entered, received, cross_in, cross_out,
    part, part_total, swap, swap_total, comb, comb_total, got, got_total, rows4,
    load_sem, exit_send, exit_recv, core_send, core_recv, z_send, z_recv,
):
    slices, cells, columns = density.shape
    lights = color.shape[1]
    z_count = view_count // 2
    stages = light_count.bit_length() - 1
    chunks = columns // LANES
    rows = got.shape[3]
    per_slice = chunks // rows
    light_step = LIGHT_DEPTH / (slices * light_count)
    view_step = VIEW_DEPTH / (cells * view_count)

    loads = [
        pltpu.make_async_copy(density_hbm.at[x], density.at[x], load_sem.at[x]) for x in range(slices)
    ] + [
        pltpu.make_async_copy(src, dst, load_sem.at[slices + i])
        for i, (src, dst) in enumerate(
            ((flip_hbm, flips), (albedo_hbm, albedo), (shift_hbm, lateral), (color_hbm, color))
        )
    ]
    for load in loads:
        load.start()

    me_light = lax.axis_index("light")
    me_view = lax.axis_index("view")
    core = lax.rem(me_view, 2)
    z = lax.div(me_view, 2)
    other = 1 - core

    def partner(b):
        bit = lax.rem(lax.div(me_light, 2**b), 2)
        return me_light + (1 - 2 * bit) * 2**b

    barrier = pltpu.get_barrier_semaphore()
    for b in range(stages):
        pl.semaphore_signal(barrier, inc=1, device_id=(partner(b), me_view), device_id_type=MESH)
    pl.semaphore_signal(barrier, inc=1, device_id=(me_light, z * 2 + other), device_id_type=MESH)
    for step in range(1, z_count):
        pl.semaphore_signal(barrier, inc=1, device_id=(me_light, lax.rem(z + step, z_count) * 2 + core), device_id_type=MESH)

    ones = jnp.ones((chunks, cells, LANES), jnp.float32)
    chain = [ones] * 3
    for x in range(slices):
        loads[x].wait()
        ext = jnp.exp(-chunked(density[x]) * light_step)
        for a, amount in enumerate(SHIFTS):
            ahead_of[a, x] = chain[a]
            chain[a] = slide(chain[a] * ext, amount, 1.0)
    for a in range(3):
        totals[a, 0] = chain[a]
        entered[a] = ones

    pl.semaphore_wait(barrier, stages + 1 + z_count - 1)

    def facts(b):
        bit = lax.rem(lax.div(me_light, 2**b), 2)
        upward = lax.div(me_light, 2 ** (b + 1)) != light_count // 2 ** (b + 1) - 1
        return bit, upward

    def exit_copy(a, b):
        return pltpu.make_async_remote_copy(
            src_ref=totals.at[a, b, low], dst_ref=received.at[a, b, low],
            send_sem=exit_send.at[a, b], recv_sem=exit_recv.at[a, b],
            device_id=(partner(b), me_view), device_id_type=MESH,
        )

    half = chunks // 2
    crossed = stages == 2 and chunks % 2 == 0 and 3 * slices <= LANES
    reach = half + 1 if crossed else chunks
    low = pl.ds(0, reach)
    high = pl.ds(chunks - reach, reach)

    def cross_copy(a, b):
        return pltpu.make_async_remote_copy(
            src_ref=totals.at[a, 0, high] if b == 0 else cross_out.at[a], dst_ref=cross_in.at[a, b],
            send_sem=exit_send.at[a, stages + b], recv_sem=exit_recv.at[a, stages + b],
            device_id=(partner(1 - b), me_view), device_id_type=MESH,
        )

    def cross_first(a):
        @pl.when(me_light < 2)
        def _():
            cross_copy(a, 0).start()

        @pl.when(me_light == 0)
        def _():
            cross_out[a] = totals[a, 0, high]
            cross_copy(a, 1).start()

    def cross_second(a):
        @pl.when(me_light >= 2)
        def _():
            cross_copy(a, 0).wait_recv()
            came = cross_in[a, 0]
            joined = slide(came, SHIFTS[a] * slices * 2, 1.0) * totals[a, 0, high]
            cross_out[a] = jnp.where(me_light == 2, joined, came)
            cross_copy(a, 1).start()

    def cross_end(a):
        @pl.when(me_light >= 1)
        def _():
            cross_copy(a, 1).wait_recv()
            entered[a, half:] = cross_in[a, 1, 1:]

        @pl.when(me_light >= 2)
        def _():
            moved = slide(cross_in[a, 0], SHIFTS[a] * slices, 1.0) * cross_in[a, 1]
            entered[a, half:] = moved[1:]

    def cross_drain(a):
        @pl.when(me_light < 2)
        def _():
            cross_copy(a, 0).wait_send()

        @pl.when(me_light != 1)
        def _():
            cross_copy(a, 1).wait_send()

    def send_exit(a, b):
        bit, upward = facts(b)

        @pl.when((bit == 0) | upward)
        def _():
            exit_copy(a, b).start()

    def advance(a, b):
        amount = SHIFTS[a]
        bit, upward = facts(b)

        @pl.when((bit == 1) | upward)
        def _():
            exit_copy(a, b).wait_recv()

        @pl.when(bit == 1)
        def _():
            moved = received[a, b, low]
            for k in range(b):
                inner = lax.rem(lax.div(me_light, 2**k), 2)
                moved = jnp.where(inner == 1, slide(moved, amount * slices * 2**k, 1.0), moved)
            entered[a, low] = moved * entered[a, low]

        if b + 1 < stages:

            @pl.when(upward)
            def _():
                mine, theirs = totals[a, b, low], received[a, b, low]
                lower = jnp.where(bit == 1, theirs, mine)
                upper = jnp.where(bit == 1, mine, theirs)
                totals[a, b + 1, low] = slide(lower, amount * slices * 2**b, 1.0) * upper

            send_exit(a, b + 1)

    for a in range(3):
        send_exit(a, 0)
        if crossed:
            cross_first(a)

    loads[slices].wait()
    loads[slices + 1].wait()
    cell = lax.broadcasted_iota(jnp.int32, (chunks, cells, LANES), 1)
    for x in range(slices):
        depth = chunked(density[x]) * view_step
        running = depth
        for step in (1, 2, 4):
            running = running + jnp.where(cell >= step, pltpu.roll(running, step, 1), 0.0)
        column = jnp.broadcast_to(running[:, cells - 1 :, :], running.shape)
        ahead = jnp.where(flips[x] == 1, column - running, running - depth)
        weight = jnp.exp(-ahead) * (1.0 - jnp.exp(-depth))
        for c in range(3):
            tinted[c, x] = weight * chunked(albedo[c, x].astype(jnp.float32))
        total = column_sums(depth)
        for j in range(per_slice):
            piece = x * per_slice + j
            part_total[piece % 2, piece // 2] = total[j * rows : (j + 1) * rows]

    def core_copy(src, dst, index):
        return pltpu.make_async_remote_copy(
            src_ref=src, dst_ref=dst, send_sem=core_send.at[index], recv_sem=core_recv.at[index],
            device_id=(me_light, z * 2 + other), device_id_type=MESH,
        )

    total_swap = core_copy(part_total.at[other], swap_total, 3)
    total_swap.start()

    def z_copy(src, dst, index, step):
        return pltpu.make_async_remote_copy(
            src_ref=src, dst_ref=dst, send_sem=z_send.at[index, step], recv_sem=z_recv.at[index, z],
            device_id=(me_light, lax.rem(z + step, z_count) * 2 + core), device_id_type=MESH,
        )

    def z_wait(dst, index, step):
        source = lax.rem(z + step, z_count)
        pltpu.make_async_remote_copy(
            src_ref=dst.at[source], dst_ref=dst.at[source], send_sem=z_send.at[index, step],
            recv_sem=z_recv.at[index, source], device_id=(me_light, source * 2 + core), device_id_type=MESH,
        ).wait_recv()

    def flip_of(piece):
        return flips[lax.div(piece, per_slice)]

    sends = []
    swaps = []

    def share_totals():
        total_swap.wait_recv()
        comb_total[...] = part_total[core] + swap_total[...]
        for step in range(1, z_count):
            copy = z_copy(comb_total.at[lax.rem(z + step, z_count)], got_total.at[z], 3, step)
            copy.start()
            sends.append(copy)
        got_total[z] = comb_total[z]
        for target in range(z_count):
            mine_first = flip_of(target * 2 + core) == core
            mine, theirs = part_total[core, target], swap_total[target]
            part_total[core, target] = jnp.where(mine_first, 1.0, jnp.exp(-theirs))
            swap_total[target] = jnp.where(mine_first, jnp.exp(-mine), 1.0)

    def march(a):
        entering = entered[a]
        for x in range(slices):
            trans = slide(entering, SHIFTS[a] * x, 1.0) * ahead_of[a, x]
            for c in range(3):
                sums = column_sums(trans * tinted[c, x])
                for j in range(per_slice):
                    piece = x * per_slice + j
                    part[a, piece % 2, piece // 2, c] = sums[j * rows : (j + 1) * rows]
        copy = core_copy(part.at[a, other], swap.at[a], a)
        copy.start()
        swaps.append(copy)

    def finish_swap(a):
        swaps[a].wait_recv()
        for target in range(z_count):
            mine_fade, their_fade = part_total[core, target], swap_total[target]
            for c in range(3):
                comb[a, target, c] = mine_fade * part[a, core, target, c] + their_fade * swap[a, target, c]
        for step in range(1, z_count):
            copy = z_copy(comb.at[a, lax.rem(z + step, z_count)], got.at[a, z], a, step)
            copy.start()
            sends.append(copy)
        got[a, z] = comb[a, z]

    for b in range(stages - 1):
        for a in range(3):
            advance(a, b)
            if crossed:
                cross_second(a)
    share_totals()
    for a in range(3):
        if stages:
            advance(a, stages - 1)
        if crossed:
            cross_end(a)
        march(a)
        if a > 0:
            finish_swap(a - 1)
    finish_swap(2)

    loads[slices + 2].wait()
    loads[slices + 3].wait()
    for step in range(1, z_count):
        z_wait(got_total, 3, step)
    flip = flip_of(me_view)
    before = jnp.zeros(got_total.shape[1:], jnp.float32)
    fades = []
    for source in range(z_count):
        fades.append(before)
        before = before + got_total[source]
    for source in range(z_count):
        depth = jnp.where(flip == 1, before - fades[source] - got_total[source], fades[source])
        fades[source] = jnp.exp(-depth)
    opacity = 1.0 - jnp.exp(-before)
    for a in range(3):
        for step in range(1, z_count):
            z_wait(got.at[a], a, step)
        for c in range(3):
            value = fades[0] * got[a, 0, c]
            for source in range(1, z_count):
                value = value + fades[source] * got[a, source, c]
            rows4[a, pl.ds(c, rows, stride=4), :] = value
        rows4[a, pl.ds(3, rows, stride=4), :] = opacity
    field = lax.rem(lax.broadcasted_iota(jnp.int32, rows4.shape[1:], 0), 4)
    for light in range(lights):
        step = lateral[light]
        picked = jnp.where(step == SHIFTS[2], rows4[2], jnp.where(step == SHIFTS[0], rows4[0], rows4[1]))
        tint = jnp.where(
            field == 0, color[0, light], jnp.where(field == 1, color[1, light], jnp.where(field == 2, color[2, light], 1.0))
        )
        lit = picked * tint
        for r in range(rows):
            out_ref[light, :, r * LANES : (r + 1) * LANES] = lit[r * 4 : (r + 1) * 4, :]

    for copy in sends:
        copy.wait_send()
    for copy in swaps:
        copy.wait_send()
    total_swap.wait_send()
    for b in range(stages):
        bit, upward = facts(b)

        @pl.when((bit == 0) | upward)
        def _():
            for a in range(3):
                exit_copy(a, b).wait_send()
    if crossed:
        for a in range(3):
            cross_drain(a)


def local(density, albedo, light_color, light_shift, view_flip):
    slices, cells, columns = density.shape
    lights = light_shift.shape[0]
    light_count = lax.axis_size("light")
    view_count = lax.axis_size("view")
    z_count = view_count // 2
    stages = light_count.bit_length() - 1
    chunks = columns // LANES
    piece = slices * columns // view_count
    rows = piece // LANES
    f32 = jnp.float32
    anywhere = pl.BlockSpec(memory_space=pl.ANY)
    dma = pltpu.SemaphoreType.DMA
    return pl.pallas_call(
        functools.partial(kernel, light_count, view_count),
        out_shape=jax.ShapeDtypeStruct((lights, 4, piece), f32),
        in_specs=[anywhere] * 5,
        out_specs=pl.BlockSpec(memory_space=pltpu.VMEM),
        scratch_shapes=[
            pltpu.VMEM(density.shape, f32),
            pltpu.VMEM(albedo.shape, albedo.dtype),
            pltpu.SMEM((3, lights), f32),
            pltpu.SMEM((lights,), jnp.int32),
            pltpu.SMEM((slices,), jnp.int32),
            pltpu.VMEM((3, slices, chunks, cells, LANES), f32),
            pltpu.VMEM((3, slices, chunks, cells, LANES), f32),
            pltpu.VMEM((3, stages, chunks, cells, LANES), f32),
            pltpu.VMEM((3, chunks, cells, LANES), f32),
            pltpu.VMEM((3, stages, chunks, cells, LANES), f32),
            pltpu.VMEM((3, 2, chunks // 2 + 1, cells, LANES), f32),
            pltpu.VMEM((3, chunks // 2 + 1, cells, LANES), f32),
            pltpu.VMEM((3, 2, z_count, 3, rows, LANES), f32),
            pltpu.VMEM((2, z_count, rows, LANES), f32),
            pltpu.VMEM((3, z_count, 3, rows, LANES), f32),
            pltpu.VMEM((z_count, rows, LANES), f32),
            pltpu.VMEM((3, z_count, 3, rows, LANES), f32),
            pltpu.VMEM((z_count, rows, LANES), f32),
            pltpu.VMEM((3, z_count, 3, rows, LANES), f32),
            pltpu.VMEM((z_count, rows, LANES), f32),
            pltpu.VMEM((3, rows * 4, LANES), f32),
            dma((slices + 4,)),
            dma((3, stages + 2)),
            dma((3, stages + 2)),
            dma((4,)),
            dma((4,)),
            dma((4, z_count)),
            dma((4, z_count)),
        ],
        compiler_params=pltpu.CompilerParams(
            collective_id=0, has_side_effects=True, vmem_limit_bytes=53 * 2**20 + 2**19
        ),
    )(density, albedo, light_color.T, light_shift, view_flip)


def solution(mesh):
    return jax.shard_map(
        local,
        mesh=mesh,
        in_specs=(P("light", "view", None), P(None, "light", "view", None), P(), P(), P("light")),
        out_specs=P(None, None, ("light", "view")),
        check_vma=False,
    )
```

```python
import functools
import jax
import jax.numpy as jnp
from jax import lax
from jax.experimental import pallas as pl
from jax.experimental.pallas import tpu as pltpu
from jax.sharding import PartitionSpec as P

LIGHT_DEPTH = 1.5
VIEW_DEPTH = 2.0
LANES = 128
SUB = 8
SHIFTS = (-1, 0, 1)
MESH = pl.DeviceIdType.MESH


def chunked(plane):
    return jnp.stack([plane[:, k : k + LANES] for k in range(0, plane.shape[1], LANES)])


def slide(planes, amount, fill):
    if amount == 0:
        return planes
    count = planes.shape[0]
    whole, part = divmod(abs(amount), LANES)
    whole = min(whole, count)
    lane = lax.broadcasted_iota(jnp.int32, planes.shape, 2)

    def blocks(n):
        return [jnp.full((n,) + planes.shape[1:], fill, planes.dtype)] if n else []

    if amount > 0:
        if whole:
            planes = jnp.concatenate(blocks(whole) + [planes[: count - whole]] * (whole < count), axis=0)
        if part:
            turned = pltpu.roll(planes, part, 2)
            before = jnp.concatenate(blocks(1) + [turned[:-1]], axis=0)
            planes = jnp.where(lane < part, before, turned)
    else:
        if whole:
            planes = jnp.concatenate([planes[whole:]] * (whole < count) + blocks(whole), axis=0)
        if part:
            turned = pltpu.roll(planes, LANES - part, 2)
            after = jnp.concatenate([turned[1:]] + blocks(1), axis=0)
            planes = jnp.where(lane >= LANES - part, after, turned)
    return planes


def column_sums(planes):
    for bit in (1, 2, 4):
        pairs = planes.reshape(planes.shape[0] // 2, 2, SUB, LANES)
        even, odd = pairs[:, 0], pairs[:, 1]
        row = lax.broadcasted_iota(jnp.int32, even.shape, 1)
        first = (row & bit) == 0
        planes = jnp.where(first, even, odd) + pltpu.roll(jnp.where(first, odd, even), SUB - bit, 1)
    return planes.reshape(planes.shape[0] * SUB, LANES)


def kernel(
    light_count, view_count, density_hbm, albedo_hbm, color_hbm, shift_hbm, flip_hbm, out_ref,
    density, albedo, color, lateral, flips, ahead_of, tinted, totals, entered, received, cross_in, cross_out,
    part, part_total, swap, swap_total, comb, comb_total, got, got_total, rows4,
    load_sem, exit_send, exit_recv, core_send, core_recv, z_send, z_recv,
):
    slices, cells, columns = density.shape
    lights = color.shape[1]
    z_count = view_count // 2
    stages = light_count.bit_length() - 1
    chunks = columns // LANES
    rows = got.shape[3]
    per_slice = chunks // rows
    light_step = LIGHT_DEPTH / (slices * light_count)
    view_step = VIEW_DEPTH / (cells * view_count)

    loads = [
        pltpu.make_async_copy(density_hbm.at[x], density.at[x], load_sem.at[x]) for x in range(slices)
    ] + [
        pltpu.make_async_copy(src, dst, load_sem.at[slices + i])
        for i, (src, dst) in enumerate(
            ((flip_hbm, flips), (albedo_hbm, albedo), (shift_hbm, lateral), (color_hbm, color))
        )
    ]
    for load in loads:
        load.start()

    me_light = lax.axis_index("light")
    me_view = lax.axis_index("view")
    core = lax.rem(me_view, 2)
    z = lax.div(me_view, 2)
    other = 1 - core

    def partner(b):
        bit = lax.rem(lax.div(me_light, 2**b), 2)
        return me_light + (1 - 2 * bit) * 2**b

    barrier = pltpu.get_barrier_semaphore()
    for b in range(stages):
        pl.semaphore_signal(barrier, inc=1, device_id=(partner(b), me_view), device_id_type=MESH)
    pl.semaphore_signal(barrier, inc=1, device_id=(me_light, z * 2 + other), device_id_type=MESH)
    for step in range(1, z_count):
        pl.semaphore_signal(barrier, inc=1, device_id=(me_light, lax.rem(z + step, z_count) * 2 + core), device_id_type=MESH)

    ones = jnp.ones((chunks, cells, LANES), jnp.float32)
    chain = [ones] * 3
    for x in range(slices):
        loads[x].wait()
        ext = jnp.exp(-chunked(density[x]) * light_step)
        for a, amount in enumerate(SHIFTS):
            ahead_of[a, x] = chain[a]
            chain[a] = slide(chain[a] * ext, amount, 1.0)
    for a in range(3):
        totals[a, 0] = chain[a]
        entered[a] = ones

    pl.semaphore_wait(barrier, stages + 1 + z_count - 1)

    def facts(b):
        bit = lax.rem(lax.div(me_light, 2**b), 2)
        upward = lax.div(me_light, 2 ** (b + 1)) != light_count // 2 ** (b + 1) - 1
        return bit, upward

    def exit_copy(a, b):
        return pltpu.make_async_remote_copy(
            src_ref=totals.at[a, b, low], dst_ref=received.at[a, b, low],
            send_sem=exit_send.at[a, b], recv_sem=exit_recv.at[a, b],
            device_id=(partner(b), me_view), device_id_type=MESH,
        )

    half = chunks // 2
    crossed = stages == 2 and chunks % 2 == 0 and 3 * slices <= LANES
    reach = half + 1 if crossed else chunks
    low = pl.ds(0, reach)
    high = pl.ds(chunks - reach, reach)

    def cross_copy(a, b):
        return pltpu.make_async_remote_copy(
            src_ref=totals.at[a, 0, high] if b == 0 else cross_out.at[a], dst_ref=cross_in.at[a, b],
            send_sem=exit_send.at[a, stages + b], recv_sem=exit_recv.at[a, stages + b],
            device_id=(partner(1 - b), me_view), device_id_type=MESH,
        )

    def cross_first(a):
        @pl.when(me_light < 2)
        def _():
            cross_copy(a, 0).start()

        @pl.when(me_light == 0)
        def _():
            cross_out[a] = totals[a, 0, high]
            cross_copy(a, 1).start()

    def cross_second(a):
        @pl.when(me_light >= 2)
        def _():
            cross_copy(a, 0).wait_recv()
            came = cross_in[a, 0]
            joined = slide(came, SHIFTS[a] * slices * 2, 1.0) * totals[a, 0, high]
            cross_out[a] = jnp.where(me_light == 2, joined, came)
            cross_copy(a, 1).start()

    def cross_end(a):
        @pl.when(me_light >= 1)
        def _():
            cross_copy(a, 1).wait_recv()
            entered[a, half:] = cross_in[a, 1, 1:]

        @pl.when(me_light >= 2)
        def _():
            moved = slide(cross_in[a, 0], SHIFTS[a] * slices, 1.0) * cross_in[a, 1]
            entered[a, half:] = moved[1:]

    def cross_drain(a):
        @pl.when(me_light < 2)
        def _():
            cross_copy(a, 0).wait_send()

        @pl.when(me_light != 1)
        def _():
            cross_copy(a, 1).wait_send()

    def send_exit(a, b):
        bit, upward = facts(b)

        @pl.when((bit == 0) | upward)
        def _():
            exit_copy(a, b).start()

    def advance(a, b):
        amount = SHIFTS[a]
        bit, upward = facts(b)

        @pl.when((bit == 1) | upward)
        def _():
            exit_copy(a, b).wait_recv()

        @pl.when(bit == 1)
        def _():
            moved = received[a, b, low]
            for k in range(b):
                inner = lax.rem(lax.div(me_light, 2**k), 2)
                moved = jnp.where(inner == 1, slide(moved, amount * slices * 2**k, 1.0), moved)
            entered[a, low] = moved * entered[a, low]

        if b + 1 < stages:

            @pl.when(upward)
            def _():
                mine, theirs = totals[a, b, low], received[a, b, low]
                lower = jnp.where(bit == 1, theirs, mine)
                upper = jnp.where(bit == 1, mine, theirs)
                totals[a, b + 1, low] = slide(lower, amount * slices * 2**b, 1.0) * upper

            send_exit(a, b + 1)

    for a in range(3):
        send_exit(a, 0)
        if crossed:
            cross_first(a)

    loads[slices].wait()
    loads[slices + 1].wait()
    cell = lax.broadcasted_iota(jnp.int32, (chunks, cells, LANES), 1)
    for x in range(slices):
        depth = chunked(density[x]) * view_step
        running = depth
        for step in (1, 2, 4):
            running = running + jnp.where(cell >= step, pltpu.roll(running, step, 1), 0.0)
        column = jnp.broadcast_to(running[:, cells - 1 :, :], running.shape)
        ahead = jnp.where(flips[x] == 1, column - running, running - depth)
        weight = jnp.exp(-ahead) * (1.0 - jnp.exp(-depth))
        for c in range(3):
            tinted[c, x] = weight * chunked(albedo[c, x].astype(jnp.float32))
        total = column_sums(depth)
        for j in range(per_slice):
            piece = x * per_slice + j
            part_total[piece % 2, piece // 2] = total[j * rows : (j + 1) * rows]

    def core_copy(src, dst, index):
        return pltpu.make_async_remote_copy(
            src_ref=src, dst_ref=dst, send_sem=core_send.at[index], recv_sem=core_recv.at[index],
            device_id=(me_light, z * 2 + other), device_id_type=MESH,
        )

    total_swap = core_copy(part_total.at[other], swap_total, 3)
    total_swap.start()

    def z_copy(src, dst, index, step):
        return pltpu.make_async_remote_copy(
            src_ref=src, dst_ref=dst, send_sem=z_send.at[index, step], recv_sem=z_recv.at[index, z],
            device_id=(me_light, lax.rem(z + step, z_count) * 2 + core), device_id_type=MESH,
        )

    def z_wait(dst, index, step):
        source = lax.rem(z + step, z_count)
        pltpu.make_async_remote_copy(
            src_ref=dst.at[source], dst_ref=dst.at[source], send_sem=z_send.at[index, step],
            recv_sem=z_recv.at[index, source], device_id=(me_light, source * 2 + core), device_id_type=MESH,
        ).wait_recv()

    def flip_of(piece):
        return flips[lax.div(piece, per_slice)]

    sends = []
    swaps = []

    def share_totals():
        total_swap.wait_recv()
        comb_total[...] = part_total[core] + swap_total[...]
        for step in range(1, z_count):
            copy = z_copy(comb_total.at[lax.rem(z + step, z_count)], got_total.at[z], 3, step)
            copy.start()
            sends.append(copy)
        got_total[z] = comb_total[z]
        for target in range(z_count):
            mine_first = flip_of(target * 2 + core) == core
            mine, theirs = part_total[core, target], swap_total[target]
            part_total[core, target] = jnp.where(mine_first, 1.0, jnp.exp(-theirs))
            swap_total[target] = jnp.where(mine_first, jnp.exp(-mine), 1.0)

    def march(a):
        entering = entered[a]
        for x in range(slices):
            trans = slide(entering, SHIFTS[a] * x, 1.0) * ahead_of[a, x]
            for c in range(3):
                sums = column_sums(trans * tinted[c, x])
                for j in range(per_slice):
                    piece = x * per_slice + j
                    part[a, piece % 2, piece // 2, c] = sums[j * rows : (j + 1) * rows]
        copy = core_copy(part.at[a, other], swap.at[a], a)
        copy.start()
        swaps.append(copy)

    def finish_swap(a):
        swaps[a].wait_recv()
        for target in range(z_count):
            mine_fade, their_fade = part_total[core, target], swap_total[target]
            for c in range(3):
                comb[a, target, c] = mine_fade * part[a, core, target, c] + their_fade * swap[a, target, c]
        for step in range(1, z_count):
            copy = z_copy(comb.at[a, lax.rem(z + step, z_count)], got.at[a, z], a, step)
            copy.start()
            sends.append(copy)
        got[a, z] = comb[a, z]

    for b in range(stages - 1):
        for a in range(3):
            advance(a, b)
            if crossed:
                cross_second(a)
    share_totals()
    for a in range(3):
        if stages:
            advance(a, stages - 1)
        if crossed:
            cross_end(a)
        march(a)
        if a > 0:
            finish_swap(a - 1)
    finish_swap(2)

    loads[slices + 2].wait()
    loads[slices + 3].wait()
    for step in range(1, z_count):
        z_wait(got_total, 3, step)
    flip = flip_of(me_view)
    before = jnp.zeros(got_total.shape[1:], jnp.float32)
    fades = []
    for source in range(z_count):
        fades.append(before)
        before = before + got_total[source]
    for source in range(z_count):
        depth = jnp.where(flip == 1, before - fades[source] - got_total[source], fades[source])
        fades[source] = jnp.exp(-depth)
    opacity = 1.0 - jnp.exp(-before)
    for a in range(3):
        for step in range(1, z_count):
            z_wait(got.at[a], a, step)
        for c in range(3):
            value = fades[0] * got[a, 0, c]
            for source in range(1, z_count):
                value = value + fades[source] * got[a, source, c]
            rows4[a, pl.ds(c, rows, stride=4), :] = value
        rows4[a, pl.ds(3, rows, stride=4), :] = opacity
    field = lax.rem(lax.broadcasted_iota(jnp.int32, rows4.shape[1:], 0), 4)
    for light in range(lights):
        step = lateral[light]
        picked = jnp.where(step == SHIFTS[2], rows4[2], jnp.where(step == SHIFTS[0], rows4[0], rows4[1]))
        tint = jnp.where(
            field == 0, color[0, light], jnp.where(field == 1, color[1, light], jnp.where(field == 2, color[2, light], 1.0))
        )
        lit = picked * tint
        for r in range(rows):
            out_ref[light, :, r * LANES : (r + 1) * LANES] = lit[r * 4 : (r + 1) * 4, :]

    for copy in sends:
        copy.wait_send()
    for copy in swaps:
        copy.wait_send()
    total_swap.wait_send()
    for b in range(stages):
        bit, upward = facts(b)

        @pl.when((bit == 0) | upward)
        def _():
            for a in range(3):
                exit_copy(a, b).wait_send()
    if crossed:
        for a in range(3):
            cross_drain(a)


def local(density, albedo, light_color, light_shift, view_flip):
    slices, cells, columns = density.shape
    lights = light_shift.shape[0]
    light_count = lax.axis_size("light")
    view_count = lax.axis_size("view")
    z_count = view_count // 2
    stages = light_count.bit_length() - 1
    chunks = columns // LANES
    piece = slices * columns // view_count
    rows = piece // LANES
    f32 = jnp.float32
    anywhere = pl.BlockSpec(memory_space=pl.ANY)
    dma = pltpu.SemaphoreType.DMA
    return pl.pallas_call(
        functools.partial(kernel, light_count, view_count),
        out_shape=jax.ShapeDtypeStruct((lights, 4, piece), f32),
        in_specs=[anywhere] * 5,
        out_specs=pl.BlockSpec(memory_space=pltpu.VMEM),
        scratch_shapes=[
            pltpu.VMEM(density.shape, f32),
            pltpu.VMEM(albedo.shape, albedo.dtype),
            pltpu.SMEM((3, lights), f32),
            pltpu.SMEM((lights,), jnp.int32),
            pltpu.SMEM((slices,), jnp.int32),
            pltpu.VMEM((3, slices, chunks, cells, LANES), f32),
            pltpu.VMEM((3, slices, chunks, cells, LANES), f32),
            pltpu.VMEM((3, stages, chunks, cells, LANES), f32),
            pltpu.VMEM((3, chunks, cells, LANES), f32),
            pltpu.VMEM((3, stages, chunks, cells, LANES), f32),
            pltpu.VMEM((3, 2, chunks // 2 + 1, cells, LANES), f32),
            pltpu.VMEM((3, chunks // 2 + 1, cells, LANES), f32),
            pltpu.VMEM((3, 2, z_count, 3, rows, LANES), f32),
            pltpu.VMEM((2, z_count, rows, LANES), f32),
            pltpu.VMEM((3, z_count, 3, rows, LANES), f32),
            pltpu.VMEM((z_count, rows, LANES), f32),
            pltpu.VMEM((3, z_count, 3, rows, LANES), f32),
            pltpu.VMEM((z_count, rows, LANES), f32),
            pltpu.VMEM((3, z_count, 3, rows, LANES), f32),
            pltpu.VMEM((z_count, rows, LANES), f32),
            pltpu.VMEM((3, rows * 4, LANES), f32),
            dma((slices + 4,)),
            dma((3, stages + 2)),
            dma((3, stages + 2)),
            dma((4,)),
            dma((4,)),
            dma((4, z_count)),
            dma((4, z_count)),
        ],
        compiler_params=pltpu.CompilerParams(
            collective_id=0, has_side_effects=True, vmem_limit_bytes=32 * 2**20
        ),
    )(*(pltpu.with_memory_space_constraint(x, pltpu.HBM) for x in (density, albedo, light_color.T, light_shift, view_flip)))


def solution(mesh):
    return jax.shard_map(
        local,
        mesh=mesh,
        in_specs=(P("light", "view", None), P(None, "light", "view", None), P(), P(), P("light")),
        out_specs=P(None, None, ("light", "view")),
        check_vma=False,
    )
```

```python
import functools
import jax
import jax.numpy as jnp
from jax import lax
from jax.experimental import pallas as pl
from jax.experimental.pallas import tpu as pltpu
from jax.sharding import PartitionSpec as P

LIGHT_DEPTH = 1.5
VIEW_DEPTH = 2.0
LANES = 128
SUB = 8
SHIFTS = (-1, 0, 1)
MESH = pl.DeviceIdType.MESH


def chunked(plane):
    return jnp.stack([plane[:, k : k + LANES] for k in range(0, plane.shape[1], LANES)])


def slide(planes, amount, fill):
    if amount == 0:
        return planes
    count = planes.shape[0]
    whole, part = divmod(abs(amount), LANES)
    whole = min(whole, count)
    lane = lax.broadcasted_iota(jnp.int32, planes.shape, 2)

    def blocks(n):
        return [jnp.full((n,) + planes.shape[1:], fill, planes.dtype)] if n else []

    if amount > 0:
        if whole:
            planes = jnp.concatenate(blocks(whole) + [planes[: count - whole]] * (whole < count), axis=0)
        if part:
            turned = pltpu.roll(planes, part, 2)
            before = jnp.concatenate(blocks(1) + [turned[:-1]], axis=0)
            planes = jnp.where(lane < part, before, turned)
    else:
        if whole:
            planes = jnp.concatenate([planes[whole:]] * (whole < count) + blocks(whole), axis=0)
        if part:
            turned = pltpu.roll(planes, LANES - part, 2)
            after = jnp.concatenate([turned[1:]] + blocks(1), axis=0)
            planes = jnp.where(lane >= LANES - part, after, turned)
    return planes


def column_sums(planes):
    for bit in (1, 2, 4):
        pairs = planes.reshape(planes.shape[0] // 2, 2, SUB, LANES)
        even, odd = pairs[:, 0], pairs[:, 1]
        row = lax.broadcasted_iota(jnp.int32, even.shape, 1)
        first = (row & bit) == 0
        planes = jnp.where(first, even, odd) + pltpu.roll(jnp.where(first, odd, even), SUB - bit, 1)
    return planes.reshape(planes.shape[0] * SUB, LANES)


def kernel(
    light_count, view_count, density_hbm, albedo_hbm, color_hbm, shift_hbm, flip_hbm, out_ref,
    density, albedo, color, lateral, flips, ahead_of, tinted, totals, entered, received, cross_in, cross_out,
    part, part_total, swap, swap_total, comb, comb_total, got, got_total, rows4, relay_in, relay_out,
    load_sem, relay_recv, exit_send, exit_recv, core_send, core_recv, z_send, z_recv,
):
    slices, cells, columns = density.shape
    lights = color.shape[1]
    z_count = view_count // 2
    stages = light_count.bit_length() - 1
    chunks = columns // LANES
    rows = got.shape[3]
    per_slice = chunks // rows
    light_step = LIGHT_DEPTH / (slices * light_count)
    view_step = VIEW_DEPTH / (cells * view_count)

    loads = [
        pltpu.make_async_copy(density_hbm.at[x], density.at[x], load_sem.at[x]) for x in range(slices)
    ] + [
        pltpu.make_async_copy(src, dst, load_sem.at[slices + i])
        for i, (src, dst) in enumerate(
            ((flip_hbm, flips), (albedo_hbm, albedo), (shift_hbm, lateral), (color_hbm, color))
        )
    ]
    for load in loads:
        load.start()

    me_light = lax.axis_index("light")
    me_view = lax.axis_index("view")
    core = lax.rem(me_view, 2)
    z = lax.div(me_view, 2)
    other = 1 - core

    def partner(b):
        bit = lax.rem(lax.div(me_light, 2**b), 2)
        return me_light + (1 - 2 * bit) * 2**b

    barrier = pltpu.get_barrier_semaphore()
    for b in range(stages):
        pl.semaphore_signal(barrier, inc=1, device_id=(partner(b), me_view), device_id_type=MESH)
    pl.semaphore_signal(barrier, inc=1, device_id=(me_light, z * 2 + other), device_id_type=MESH)
    for step in range(1, z_count):
        pl.semaphore_signal(barrier, inc=1, device_id=(me_light, lax.rem(z + step, z_count) * 2 + core), device_id_type=MESH)

    ones = jnp.ones((chunks, cells, LANES), jnp.float32)
    chain = [ones] * 3
    for x in range(slices):
        loads[x].wait()
        ext = jnp.exp(-chunked(density[x]) * light_step)
        for a, amount in enumerate(SHIFTS):
            ahead_of[a, x] = chain[a]
            chain[a] = slide(chain[a] * ext, amount, 1.0)
    for a in range(3):
        totals[a, 0] = chain[a]
        entered[a] = ones

    pl.semaphore_wait(barrier, stages + 1 + z_count - 1)

    def facts(b):
        bit = lax.rem(lax.div(me_light, 2**b), 2)
        upward = lax.div(me_light, 2 ** (b + 1)) != light_count // 2 ** (b + 1) - 1
        return bit, upward

    def exit_copy(a, b):
        return pltpu.make_async_remote_copy(
            src_ref=totals.at[a, b, low], dst_ref=received.at[a, b, low],
            send_sem=exit_send.at[a, b], recv_sem=exit_recv.at[a, b],
            device_id=(partner(b), me_view), device_id_type=MESH,
        )

    half = chunks // 2
    crossed = stages == 2 and chunks % 2 == 0 and 3 * slices <= LANES
    reach = half + 1 if crossed else chunks
    low = pl.ds(0, reach)
    high = pl.ds(chunks - reach, reach)

    def cross_copy(a, b):
        return pltpu.make_async_remote_copy(
            src_ref=totals.at[a, 0, high] if b == 0 else cross_out.at[a], dst_ref=cross_in.at[a, b],
            send_sem=exit_send.at[a, stages + b], recv_sem=exit_recv.at[a, stages + b],
            device_id=(partner(1 - b), me_view), device_id_type=MESH,
        )

    def cross_first(a):
        @pl.when(me_light < 2)
        def _():
            cross_copy(a, 0).start()

        @pl.when(me_light == 0)
        def _():
            cross_out[a] = totals[a, 0, high]
            cross_copy(a, 1).start()

    def cross_second(a):
        @pl.when(me_light >= 2)
        def _():
            cross_copy(a, 0).wait_recv()
            came = cross_in[a, 0]
            joined = slide(came, SHIFTS[a] * slices * 2, 1.0) * totals[a, 0, high]
            cross_out[a] = jnp.where(me_light == 2, joined, came)
            cross_copy(a, 1).start()

    def cross_end(a):
        @pl.when(me_light >= 1)
        def _():
            cross_copy(a, 1).wait_recv()
            entered[a, half:] = cross_in[a, 1, 1:]

        @pl.when(me_light >= 2)
        def _():
            moved = slide(cross_in[a, 0], SHIFTS[a] * slices, 1.0) * cross_in[a, 1]
            entered[a, half:] = moved[1:]

    def cross_drain(a):
        @pl.when(me_light < 2)
        def _():
            cross_copy(a, 0).wait_send()

        @pl.when(me_light != 1)
        def _():
            cross_copy(a, 1).wait_send()

    def send_exit(a, b):
        bit, upward = facts(b)

        @pl.when((bit == 0) | upward)
        def _():
            exit_copy(a, b).start()

    def advance(a, b):
        amount = SHIFTS[a]
        bit, upward = facts(b)

        @pl.when((bit == 1) | upward)
        def _():
            exit_copy(a, b).wait_recv()

        @pl.when(bit == 1)
        def _():
            moved = received[a, b, low]
            for k in range(b):
                inner = lax.rem(lax.div(me_light, 2**k), 2)
                moved = jnp.where(inner == 1, slide(moved, amount * slices * 2**k, 1.0), moved)
            entered[a, low] = moved * entered[a, low]

        if b + 1 < stages:

            @pl.when(upward)
            def _():
                mine, theirs = totals[a, b, low], received[a, b, low]
                lower = jnp.where(bit == 1, theirs, mine)
                upper = jnp.where(bit == 1, mine, theirs)
                totals[a, b + 1, low] = slide(lower, amount * slices * 2**b, 1.0) * upper

            send_exit(a, b + 1)

    for a in range(3):
        send_exit(a, 0)
        if crossed:
            cross_first(a)

    loads[slices].wait()
    loads[slices + 1].wait()
    cell = lax.broadcasted_iota(jnp.int32, (chunks, cells, LANES), 1)
    for x in range(slices):
        depth = chunked(density[x]) * view_step
        running = depth
        for step in (1, 2, 4):
            running = running + jnp.where(cell >= step, pltpu.roll(running, step, 1), 0.0)
        column = jnp.broadcast_to(running[:, cells - 1 :, :], running.shape)
        ahead = jnp.where(flips[x] == 1, column - running, running - depth)
        weight = jnp.exp(-ahead) * (1.0 - jnp.exp(-depth))
        for c in range(3):
            tinted[c, x] = weight * chunked(albedo[c, x].astype(jnp.float32))
        total = column_sums(depth)
        for j in range(per_slice):
            piece = x * per_slice + j
            part_total[piece % 2, piece // 2] = total[j * rows : (j + 1) * rows]

    def core_copy(src, dst, index):
        return pltpu.make_async_remote_copy(
            src_ref=src, dst_ref=dst, send_sem=core_send.at[index], recv_sem=core_recv.at[index],
            device_id=(me_light, z * 2 + other), device_id_type=MESH,
        )

    total_swap = core_copy(part_total.at[other], swap_total, 3)
    total_swap.start()

    def z_copy(src, dst, index, step):
        return pltpu.make_async_remote_copy(
            src_ref=src, dst_ref=dst, send_sem=z_send.at[index, step], recv_sem=z_recv.at[index, z],
            device_id=(me_light, lax.rem(z + step, z_count) * 2 + core), device_id_type=MESH,
        )

    def z_wait(dst, index, step):
        source = lax.rem(z + step, z_count)
        pltpu.make_async_remote_copy(
            src_ref=dst.at[source], dst_ref=dst.at[source], send_sem=z_send.at[index, step],
            recv_sem=z_recv.at[index, source], device_id=(me_light, source * 2 + core), device_id_type=MESH,
        ).wait_recv()

    relayed = z_count >= 4

    def far(step):
        if not relayed or step not in (1, z_count - 1):
            return False
        return z == (0 if step == z_count - 1 else z_count - 1)

    def late(step):
        if not relayed or step not in (2, z_count - 2):
            return False
        from_low = (z == 1) if step == z_count - 2 else False
        from_high = (z == z_count - 2) if step == 2 else False
        return from_low | from_high

    def relay_copy(src, index, step):
        return pltpu.make_async_remote_copy(
            src_ref=src, dst_ref=relay_in.at[3, 0] if index == 3 else relay_in.at[index], send_sem=z_send.at[index, step], recv_sem=relay_recv.at[index],
            device_id=(me_light, (z + 1 - 2 * lax.div(z, z_count - 1)) * 2 + core), device_id_type=MESH,
        )

    def spread(pieces, dst, index):
        for step in range(1, z_count):
            target = lax.rem(z + step, z_count)
            copy = z_copy(pieces.at[target], dst.at[z], index, step)
            is_far, is_late = far(step), late(step)
            if is_far is False and is_late is False:
                copy.start()
            else:
                if is_far is not False:

                    @pl.when(is_far)
                    def _():
                        relay_copy(pieces.at[target], index, step).start()

                @pl.when(jnp.logical_not(is_far | is_late))
                def _():
                    copy.start()

            sends.append(copy)

    def relay(index):
        if not relayed:
            return
        for step in sorted({2, z_count - 2}):

            @pl.when(late(step))
            def _():
                target = lax.rem(z + step, z_count)
                relay_copy(relay_in.at[3, 0] if index == 3 else relay_in.at[index], index, step).wait_recv()
                if index == 3:
                    theirs, mine = relay_in[3, 0], comb_total[target]
                    relay_out[3, 0] = mine + theirs
                    mine_first = flip_of(target * 2 + core) == (z == 1).astype(jnp.int32)
                    relay_out[3, 1] = jnp.where(mine_first, 1.0, jnp.exp(-theirs))
                    relay_out[3, 2] = jnp.where(mine_first, jnp.exp(-mine), 1.0)
                    z_copy(relay_out.at[3, 0], got_total.at[z], 3, step).start()
                else:
                    for c in range(3):
                        relay_out[index, c] = (
                            relay_out[3, 1] * comb[index, target, c] + relay_out[3, 2] * relay_in[index, c]
                        )
                    z_copy(relay_out.at[index], got.at[index, z], index, step).start()

    def z_arrive(dst, index, step):
        is_far = far(step)
        if is_far is False:
            z_wait(dst, index, step)
        else:

            @pl.when(jnp.logical_not(is_far))
            def _():
                z_wait(dst, index, step)

            @pl.when(is_far)
            def _():
                source = lax.rem(z + step, z_count)
                dst[source] = jnp.zeros(dst.shape[1:], jnp.float32)

    def flip_of(piece):
        return flips[lax.div(piece, per_slice)]

    sends = []
    swaps = []

    def share_totals():
        total_swap.wait_recv()
        comb_total[...] = part_total[core] + swap_total[...]
        spread(comb_total, got_total, 3)
        got_total[z] = comb_total[z]
        for target in range(z_count):
            mine_first = flip_of(target * 2 + core) == core
            mine, theirs = part_total[core, target], swap_total[target]
            part_total[core, target] = jnp.where(mine_first, 1.0, jnp.exp(-theirs))
            swap_total[target] = jnp.where(mine_first, jnp.exp(-mine), 1.0)

    def march(a):
        entering = entered[a]
        for x in range(slices):
            trans = slide(entering, SHIFTS[a] * x, 1.0) * ahead_of[a, x]
            for c in range(3):
                sums = column_sums(trans * tinted[c, x])
                for j in range(per_slice):
                    piece = x * per_slice + j
                    part[a, piece % 2, piece // 2, c] = sums[j * rows : (j + 1) * rows]
        copy = core_copy(part.at[a, other], swap.at[a], a)
        copy.start()
        swaps.append(copy)

    def finish_swap(a):
        swaps[a].wait_recv()
        for target in range(z_count):
            mine_fade, their_fade = part_total[core, target], swap_total[target]
            for c in range(3):
                comb[a, target, c] = mine_fade * part[a, core, target, c] + their_fade * swap[a, target, c]
        spread(comb.at[a], got.at[a], a)
        got[a, z] = comb[a, z]

    for b in range(stages - 1):
        for a in range(3):
            advance(a, b)
            if crossed:
                cross_second(a)
    share_totals()
    for a in range(3):
        if stages:
            advance(a, stages - 1)
        if crossed:
            cross_end(a)
        march(a)
        if a == 0:
            relay(3)
        else:
            finish_swap(a - 1)
        if a > 1:
            relay(a - 2)
    finish_swap(2)
    relay(1)
    relay(2)

    loads[slices + 2].wait()
    loads[slices + 3].wait()
    for step in range(1, z_count):
        z_arrive(got_total, 3, step)
    flip = flip_of(me_view)
    before = jnp.zeros(got_total.shape[1:], jnp.float32)
    fades = []
    for source in range(z_count):
        fades.append(before)
        before = before + got_total[source]
    for source in range(z_count):
        depth = jnp.where(flip == 1, before - fades[source] - got_total[source], fades[source])
        fades[source] = jnp.exp(-depth)
    opacity = 1.0 - jnp.exp(-before)
    for a in range(3):
        for step in range(1, z_count):
            z_arrive(got.at[a], a, step)
        for c in range(3):
            value = fades[0] * got[a, 0, c]
            for source in range(1, z_count):
                value = value + fades[source] * got[a, source, c]
            rows4[a, pl.ds(c, rows, stride=4), :] = value
        rows4[a, pl.ds(3, rows, stride=4), :] = opacity
    field = lax.rem(lax.broadcasted_iota(jnp.int32, rows4.shape[1:], 0), 4)
    for light in range(lights):
        step = lateral[light]
        picked = jnp.where(step == SHIFTS[2], rows4[2], jnp.where(step == SHIFTS[0], rows4[0], rows4[1]))
        tint = jnp.where(
            field == 0, color[0, light], jnp.where(field == 1, color[1, light], jnp.where(field == 2, color[2, light], 1.0))
        )
        lit = picked * tint
        for r in range(rows):
            out_ref[light, :, r * LANES : (r + 1) * LANES] = lit[r * 4 : (r + 1) * 4, :]

    for copy in sends:
        copy.wait_send()
    for copy in swaps:
        copy.wait_send()
    total_swap.wait_send()
    for b in range(stages):
        bit, upward = facts(b)

        @pl.when((bit == 0) | upward)
        def _():
            for a in range(3):
                exit_copy(a, b).wait_send()
    if crossed:
        for a in range(3):
            cross_drain(a)


def local(density, albedo, light_color, light_shift, view_flip):
    slices, cells, columns = density.shape
    lights = light_shift.shape[0]
    light_count = lax.axis_size("light")
    view_count = lax.axis_size("view")
    z_count = view_count // 2
    stages = light_count.bit_length() - 1
    chunks = columns // LANES
    piece = slices * columns // view_count
    rows = piece // LANES
    f32 = jnp.float32
    anywhere = pl.BlockSpec(memory_space=pl.ANY)
    dma = pltpu.SemaphoreType.DMA
    return pl.pallas_call(
        functools.partial(kernel, light_count, view_count),
        out_shape=jax.ShapeDtypeStruct((lights, 4, piece), f32),
        in_specs=[anywhere] * 5,
        out_specs=pl.BlockSpec(memory_space=pltpu.VMEM),
        scratch_shapes=[
            pltpu.VMEM(density.shape, f32),
            pltpu.VMEM(albedo.shape, albedo.dtype),
            pltpu.SMEM((3, lights), f32),
            pltpu.SMEM((lights,), jnp.int32),
            pltpu.SMEM((slices,), jnp.int32),
            pltpu.VMEM((3, slices, chunks, cells, LANES), f32),
            pltpu.VMEM((3, slices, chunks, cells, LANES), f32),
            pltpu.VMEM((3, stages, chunks, cells, LANES), f32),
            pltpu.VMEM((3, chunks, cells, LANES), f32),
            pltpu.VMEM((3, stages, chunks, cells, LANES), f32),
            pltpu.VMEM((3, 2, chunks // 2 + 1, cells, LANES), f32),
            pltpu.VMEM((3, chunks // 2 + 1, cells, LANES), f32),
            pltpu.VMEM((3, 2, z_count, 3, rows, LANES), f32),
            pltpu.VMEM((2, z_count, rows, LANES), f32),
            pltpu.VMEM((3, z_count, 3, rows, LANES), f32),
            pltpu.VMEM((z_count, rows, LANES), f32),
            pltpu.VMEM((3, z_count, 3, rows, LANES), f32),
            pltpu.VMEM((z_count, rows, LANES), f32),
            pltpu.VMEM((3, z_count, 3, rows, LANES), f32),
            pltpu.VMEM((z_count, rows, LANES), f32),
            pltpu.VMEM((3, rows * 4, LANES), f32),
            pltpu.VMEM((4, 3, rows, LANES), f32),
            pltpu.VMEM((4, 3, rows, LANES), f32),
            dma((slices + 4,)),
            dma((4,)),
            dma((3, stages + 2)),
            dma((3, stages + 2)),
            dma((4,)),
            dma((4,)),
            dma((4, z_count)),
            dma((4, z_count)),
        ],
        compiler_params=pltpu.CompilerParams(
            collective_id=0, has_side_effects=True, vmem_limit_bytes=32 * 2**20
        ),
    )(*(pltpu.with_memory_space_constraint(x, pltpu.HBM) for x in (density, albedo, light_color.T, light_shift, view_flip)))


def solution(mesh):
    return jax.shard_map(
        local,
        mesh=mesh,
        in_specs=(P("light", "view", None), P(None, "light", "view", None), P(), P(), P("light")),
        out_specs=P(None, None, ("light", "view")),
        check_vma=False,
    )
```

```python
import functools
import jax
import jax.numpy as jnp
from jax import lax
from jax.experimental import pallas as pl
from jax.experimental.pallas import tpu as pltpu
from jax.sharding import PartitionSpec as P

LIGHT_DEPTH = 1.5
VIEW_DEPTH = 2.0
LANES = 128
SUB = 8
SHIFTS = (-1, 0, 1)
MESH = pl.DeviceIdType.MESH


def chunked(plane):
    return jnp.stack([plane[:, k : k + LANES] for k in range(0, plane.shape[1], LANES)])


def slide(planes, amount, fill):
    if amount == 0:
        return planes
    count = planes.shape[0]
    whole, part = divmod(abs(amount), LANES)
    whole = min(whole, count)
    lane = lax.broadcasted_iota(jnp.int32, planes.shape, 2)

    def blocks(n):
        return [jnp.full((n,) + planes.shape[1:], fill, planes.dtype)] if n else []

    if amount > 0:
        if whole:
            planes = jnp.concatenate(blocks(whole) + [planes[: count - whole]] * (whole < count), axis=0)
        if part:
            turned = pltpu.roll(planes, part, 2)
            before = jnp.concatenate(blocks(1) + [turned[:-1]], axis=0)
            planes = jnp.where(lane < part, before, turned)
    else:
        if whole:
            planes = jnp.concatenate([planes[whole:]] * (whole < count) + blocks(whole), axis=0)
        if part:
            turned = pltpu.roll(planes, LANES - part, 2)
            after = jnp.concatenate([turned[1:]] + blocks(1), axis=0)
            planes = jnp.where(lane >= LANES - part, after, turned)
    return planes


def column_sums(planes):
    for bit in (1, 2, 4):
        pairs = planes.reshape(planes.shape[0] // 2, 2, SUB, LANES)
        even, odd = pairs[:, 0], pairs[:, 1]
        row = lax.broadcasted_iota(jnp.int32, even.shape, 1)
        first = (row & bit) == 0
        planes = jnp.where(first, even, odd) + pltpu.roll(jnp.where(first, odd, even), SUB - bit, 1)
    return planes.reshape(planes.shape[0] * SUB, LANES)


def kernel(
    light_count, view_count, density_hbm, albedo_hbm, color_hbm, shift_hbm, flip_hbm, out_ref,
    density, albedo, color, lateral, flips, ahead_of, tinted, totals, entered, received, cross_in, cross_out,
    part, part_total, swap, swap_total, comb, comb_total, got, got_total, rows4,
    load_sem, exit_send, exit_recv, core_send, core_recv, z_send, z_recv,
):
    slices, cells, columns = density.shape
    lights = color.shape[1]
    z_count = view_count // 2
    stages = light_count.bit_length() - 1
    chunks = columns // LANES
    rows = got.shape[3]
    per_slice = chunks // rows
    light_step = LIGHT_DEPTH / (slices * light_count)
    view_step = VIEW_DEPTH / (cells * view_count)

    loads = [
        pltpu.make_async_copy(density_hbm.at[x], density.at[x], load_sem.at[x]) for x in range(slices)
    ] + [
        pltpu.make_async_copy(src, dst, load_sem.at[slices + i])
        for i, (src, dst) in enumerate(
            ((flip_hbm, flips), (albedo_hbm, albedo), (shift_hbm, lateral), (color_hbm, color))
        )
    ]
    for load in loads:
        load.start()

    me_light = lax.axis_index("light")
    me_view = lax.axis_index("view")
    core = lax.rem(me_view, 2)
    z = lax.div(me_view, 2)
    other = 1 - core

    def partner(b):
        bit = lax.rem(lax.div(me_light, 2**b), 2)
        return me_light + (1 - 2 * bit) * 2**b

    barrier = pltpu.get_barrier_semaphore()
    for b in range(stages):
        pl.semaphore_signal(barrier, inc=1, device_id=(partner(b), me_view), device_id_type=MESH)
    pl.semaphore_signal(barrier, inc=1, device_id=(me_light, z * 2 + other), device_id_type=MESH)
    for step in range(1, z_count):
        pl.semaphore_signal(barrier, inc=1, device_id=(me_light, lax.rem(z + step, z_count) * 2 + core), device_id_type=MESH)

    ones = jnp.ones((chunks, cells, LANES), jnp.float32)
    chain = [ones] * 3
    for x in range(slices):
        loads[x].wait()
        ext = jnp.exp(-chunked(density[x]) * light_step)
        for a, amount in enumerate(SHIFTS):
            ahead_of[a, x] = chain[a]
            chain[a] = slide(chain[a] * ext, amount, 1.0)
    for a in range(3):
        totals[a, 0] = chain[a]
        entered[a] = ones

    pl.semaphore_wait(barrier, stages + 1 + z_count - 1)

    def facts(b):
        bit = lax.rem(lax.div(me_light, 2**b), 2)
        upward = lax.div(me_light, 2 ** (b + 1)) != light_count // 2 ** (b + 1) - 1
        return bit, upward

    def exit_copy(a, b):
        return pltpu.make_async_remote_copy(
            src_ref=totals.at[a, b, low], dst_ref=received.at[a, b, low],
            send_sem=exit_send.at[a, b], recv_sem=exit_recv.at[a, b],
            device_id=(partner(b), me_view), device_id_type=MESH,
        )

    half = chunks // 2
    crossed = stages == 2 and chunks % 2 == 0 and 3 * slices <= LANES
    reach = half + 1 if crossed else chunks
    low = pl.ds(0, reach)
    high = pl.ds(chunks - reach, reach)

    def cross_copy(a, b):
        return pltpu.make_async_remote_copy(
            src_ref=totals.at[a, 0, high] if b == 0 else cross_out.at[a], dst_ref=cross_in.at[a, b],
            send_sem=exit_send.at[a, stages + b], recv_sem=exit_recv.at[a, stages + b],
            device_id=(partner(1 - b), me_view), device_id_type=MESH,
        )

    def cross_first(a):
        @pl.when(me_light < 2)
        def _():
            cross_copy(a, 0).start()

        @pl.when(me_light == 0)
        def _():
            cross_out[a] = totals[a, 0, high]
            cross_copy(a, 1).start()

    def cross_second(a):
        @pl.when(me_light >= 2)
        def _():
            cross_copy(a, 0).wait_recv()
            came = cross_in[a, 0]
            joined = slide(came, SHIFTS[a] * slices * 2, 1.0) * totals[a, 0, high]
            cross_out[a] = jnp.where(me_light == 2, joined, came)
            cross_copy(a, 1).start()

    def cross_end(a):
        @pl.when(me_light >= 1)
        def _():
            cross_copy(a, 1).wait_recv()
            entered[a, half:] = cross_in[a, 1, 1:]

        @pl.when(me_light >= 2)
        def _():
            moved = slide(cross_in[a, 0], SHIFTS[a] * slices, 1.0) * cross_in[a, 1]
            entered[a, half:] = moved[1:]

    def cross_drain(a):
        @pl.when(me_light < 2)
        def _():
            cross_copy(a, 0).wait_send()

        @pl.when(me_light != 1)
        def _():
            cross_copy(a, 1).wait_send()

    def send_exit(a, b):
        bit, upward = facts(b)

        @pl.when((bit == 0) | upward)
        def _():
            exit_copy(a, b).start()

    def advance(a, b):
        amount = SHIFTS[a]
        bit, upward = facts(b)

        @pl.when((bit == 1) | upward)
        def _():
            exit_copy(a, b).wait_recv()

        @pl.when(bit == 1)
        def _():
            moved = received[a, b, low]
            for k in range(b):
                inner = lax.rem(lax.div(me_light, 2**k), 2)
                moved = jnp.where(inner == 1, slide(moved, amount * slices * 2**k, 1.0), moved)
            entered[a, low] = moved * entered[a, low]

        if b + 1 < stages:

            @pl.when(upward)
            def _():
                mine, theirs = totals[a, b, low], received[a, b, low]
                lower = jnp.where(bit == 1, theirs, mine)
                upper = jnp.where(bit == 1, mine, theirs)
                totals[a, b + 1, low] = slide(lower, amount * slices * 2**b, 1.0) * upper

            send_exit(a, b + 1)

    for a in range(3):
        send_exit(a, 0)
        if crossed:
            cross_first(a)

    loads[slices].wait()
    loads[slices + 1].wait()
    cell = lax.broadcasted_iota(jnp.int32, (chunks, cells, LANES), 1)
    for x in range(slices):
        depth = chunked(density[x]) * view_step
        running = depth
        for step in (1, 2, 4):
            running = running + jnp.where(cell >= step, pltpu.roll(running, step, 1), 0.0)
        column = jnp.broadcast_to(running[:, cells - 1 :, :], running.shape)
        ahead = jnp.where(flips[x] == 1, column - running, running - depth)
        weight = jnp.exp(-ahead) * (1.0 - jnp.exp(-depth))
        for c in range(3):
            tinted[c, x] = weight * chunked(albedo[c, x].astype(jnp.float32))
        total = column_sums(depth)
        for j in range(per_slice):
            piece = x * per_slice + j
            part_total[piece % 2, piece // 2] = total[j * rows : (j + 1) * rows]

    def core_copy(src, dst, index):
        return pltpu.make_async_remote_copy(
            src_ref=src, dst_ref=dst, send_sem=core_send.at[index], recv_sem=core_recv.at[index],
            device_id=(me_light, z * 2 + other), device_id_type=MESH,
        )

    total_swap = core_copy(part_total.at[other], swap_total, 3)
    total_swap.start()

    def z_copy(src, dst, index, step):
        return pltpu.make_async_remote_copy(
            src_ref=src, dst_ref=dst, send_sem=z_send.at[index, step], recv_sem=z_recv.at[index, z],
            device_id=(me_light, lax.rem(z + step, z_count) * 2 + core), device_id_type=MESH,
        )

    def z_wait(dst, index, step):
        source = lax.rem(z + step, z_count)
        pltpu.make_async_remote_copy(
            src_ref=dst.at[source], dst_ref=dst.at[source], send_sem=z_send.at[index, step],
            recv_sem=z_recv.at[index, source], device_id=(me_light, source * 2 + core), device_id_type=MESH,
        ).wait_recv()

    def flip_of(piece):
        return flips[lax.div(piece, per_slice)]

    sends = []
    swaps = []

    def share_totals():
        total_swap.wait_recv()
        comb_total[...] = part_total[core] + swap_total[...]
        for step in range(1, z_count):
            copy = z_copy(comb_total.at[lax.rem(z + step, z_count)], got_total.at[z], 3, step)
            copy.start()
            sends.append(copy)
        got_total[z] = comb_total[z]
        for target in range(z_count):
            mine_first = flip_of(target * 2 + core) == core
            mine, theirs = part_total[core, target], swap_total[target]
            part_total[core, target] = jnp.where(mine_first, 1.0, jnp.exp(-theirs))
            swap_total[target] = jnp.where(mine_first, jnp.exp(-mine), 1.0)

    def render(a, wanted):
        entering = entered[a]
        for x in wanted:
            trans = slide(entering, SHIFTS[a] * x, 1.0) * ahead_of[a, x]
            for c in range(3):
                sums = column_sums(trans * tinted[c, x])
                for j in range(per_slice):
                    piece = x * per_slice + j
                    part[a, piece % 2, piece // 2, c] = sums[j * rows : (j + 1) * rows]

    def render_half(a, own):
        for parity in range(2):

            @pl.when((core if own else other) == parity)
            def _():
                render(a, range(parity, slices, 2))

    def march(a):
        if per_slice == 1:
            render_half(a, False)
        else:
            render(a, range(slices))
        copy = core_copy(part.at[a, other], swap.at[a], a)
        copy.start()
        swaps.append(copy)
        if a > 0:
            finish_swap(a - 1)
        if per_slice == 1:
            render_half(a, True)

    def finish_swap(a):
        swaps[a].wait_recv()
        for target in range(z_count):
            mine_fade, their_fade = part_total[core, target], swap_total[target]
            for c in range(3):
                comb[a, target, c] = mine_fade * part[a, core, target, c] + their_fade * swap[a, target, c]
        for step in range(1, z_count):
            copy = z_copy(comb.at[a, lax.rem(z + step, z_count)], got.at[a, z], a, step)
            copy.start()
            sends.append(copy)
        got[a, z] = comb[a, z]

    for b in range(stages - 1):
        for a in range(3):
            advance(a, b)
            if crossed:
                cross_second(a)
    share_totals()
    for a in range(3):
        if stages:
            advance(a, stages - 1)
        if crossed:
            cross_end(a)
        march(a)
    finish_swap(2)

    loads[slices + 2].wait()
    loads[slices + 3].wait()
    for step in range(1, z_count):
        z_wait(got_total, 3, step)
    flip = flip_of(me_view)
    before = jnp.zeros(got_total.shape[1:], jnp.float32)
    fades = []
    for source in range(z_count):
        fades.append(before)
        before = before + got_total[source]
    for source in range(z_count):
        depth = jnp.where(flip == 1, before - fades[source] - got_total[source], fades[source])
        fades[source] = jnp.exp(-depth)
    opacity = 1.0 - jnp.exp(-before)
    for a in range(3):
        for step in range(1, z_count):
            z_wait(got.at[a], a, step)
        for c in range(3):
            value = fades[0] * got[a, 0, c]
            for source in range(1, z_count):
                value = value + fades[source] * got[a, source, c]
            rows4[a, pl.ds(c, rows, stride=4), :] = value
        rows4[a, pl.ds(3, rows, stride=4), :] = opacity
    field = lax.rem(lax.broadcasted_iota(jnp.int32, rows4.shape[1:], 0), 4)
    for light in range(lights):
        step = lateral[light]
        picked = jnp.where(step == SHIFTS[2], rows4[2], jnp.where(step == SHIFTS[0], rows4[0], rows4[1]))
        tint = jnp.where(
            field == 0, color[0, light], jnp.where(field == 1, color[1, light], jnp.where(field == 2, color[2, light], 1.0))
        )
        lit = picked * tint
        for r in range(rows):
            out_ref[light, :, r * LANES : (r + 1) * LANES] = lit[r * 4 : (r + 1) * 4, :]

    for copy in sends:
        copy.wait_send()
    for copy in swaps:
        copy.wait_send()
    total_swap.wait_send()
    for b in range(stages):
        bit, upward = facts(b)

        @pl.when((bit == 0) | upward)
        def _():
            for a in range(3):
                exit_copy(a, b).wait_send()
    if crossed:
        for a in range(3):
            cross_drain(a)


def local(density, albedo, light_color, light_shift, view_flip):
    slices, cells, columns = density.shape
    lights = light_shift.shape[0]
    light_count = lax.axis_size("light")
    view_count = lax.axis_size("view")
    z_count = view_count // 2
    stages = light_count.bit_length() - 1
    chunks = columns // LANES
    piece = slices * columns // view_count
    rows = piece // LANES
    f32 = jnp.float32
    anywhere = pl.BlockSpec(memory_space=pl.ANY)
    dma = pltpu.SemaphoreType.DMA
    return pl.pallas_call(
        functools.partial(kernel, light_count, view_count),
        out_shape=jax.ShapeDtypeStruct((lights, 4, piece), f32),
        in_specs=[anywhere] * 5,
        out_specs=pl.BlockSpec(memory_space=pltpu.VMEM),
        scratch_shapes=[
            pltpu.VMEM(density.shape, f32),
            pltpu.VMEM(albedo.shape, albedo.dtype),
            pltpu.SMEM((3, lights), f32),
            pltpu.SMEM((lights,), jnp.int32),
            pltpu.SMEM((slices,), jnp.int32),
            pltpu.VMEM((3, slices, chunks, cells, LANES), f32),
            pltpu.VMEM((3, slices, chunks, cells, LANES), f32),
            pltpu.VMEM((3, stages, chunks, cells, LANES), f32),
            pltpu.VMEM((3, chunks, cells, LANES), f32),
            pltpu.VMEM((3, stages, chunks, cells, LANES), f32),
            pltpu.VMEM((3, 2, chunks // 2 + 1, cells, LANES), f32),
            pltpu.VMEM((3, chunks // 2 + 1, cells, LANES), f32),
            pltpu.VMEM((3, 2, z_count, 3, rows, LANES), f32),
            pltpu.VMEM((2, z_count, rows, LANES), f32),
            pltpu.VMEM((3, z_count, 3, rows, LANES), f32),
            pltpu.VMEM((z_count, rows, LANES), f32),
            pltpu.VMEM((3, z_count, 3, rows, LANES), f32),
            pltpu.VMEM((z_count, rows, LANES), f32),
            pltpu.VMEM((3, z_count, 3, rows, LANES), f32),
            pltpu.VMEM((z_count, rows, LANES), f32),
            pltpu.VMEM((3, rows * 4, LANES), f32),
            dma((slices + 4,)),
            dma((3, stages + 2)),
            dma((3, stages + 2)),
            dma((4,)),
            dma((4,)),
            dma((4, z_count)),
            dma((4, z_count)),
        ],
        compiler_params=pltpu.CompilerParams(
            collective_id=0, has_side_effects=True, vmem_limit_bytes=32 * 2**20
        ),
    )(*(pltpu.with_memory_space_constraint(x, pltpu.HBM) for x in (density, albedo, light_color.T, light_shift, view_flip)))


def solution(mesh):
    return jax.shard_map(
        local,
        mesh=mesh,
        in_specs=(P("light", "view", None), P(None, "light", "view", None), P(), P(), P("light")),
        out_specs=P(None, None, ("light", "view")),
        check_vma=False,
    )
```

```python
import functools
import jax
import jax.numpy as jnp
from jax import lax
from jax.experimental import pallas as pl
from jax.experimental.pallas import tpu as pltpu
from jax.sharding import PartitionSpec as P

LIGHT_DEPTH = 1.5
VIEW_DEPTH = 2.0
LANES = 128
SUB = 8
SHIFTS = (-1, 0, 1)
MESH = pl.DeviceIdType.MESH


def chunked(plane):
    return jnp.stack([plane[:, k : k + LANES] for k in range(0, plane.shape[1], LANES)])


def slide(planes, amount, fill):
    if amount == 0:
        return planes
    count = planes.shape[0]
    whole, part = divmod(abs(amount), LANES)
    whole = min(whole, count)
    lane = lax.broadcasted_iota(jnp.int32, planes.shape, 2)

    def blocks(n):
        return [jnp.full((n,) + planes.shape[1:], fill, planes.dtype)] if n else []

    if amount > 0:
        if whole:
            planes = jnp.concatenate(blocks(whole) + [planes[: count - whole]] * (whole < count), axis=0)
        if part:
            turned = pltpu.roll(planes, part, 2)
            before = jnp.concatenate(blocks(1) + [turned[:-1]], axis=0)
            planes = jnp.where(lane < part, before, turned)
    else:
        if whole:
            planes = jnp.concatenate([planes[whole:]] * (whole < count) + blocks(whole), axis=0)
        if part:
            turned = pltpu.roll(planes, LANES - part, 2)
            after = jnp.concatenate([turned[1:]] + blocks(1), axis=0)
            planes = jnp.where(lane >= LANES - part, after, turned)
    return planes


def column_sums(planes):
    for bit in (1, 2, 4):
        pairs = planes.reshape(planes.shape[0] // 2, 2, SUB, LANES)
        even, odd = pairs[:, 0], pairs[:, 1]
        row = lax.broadcasted_iota(jnp.int32, even.shape, 1)
        first = (row & bit) == 0
        planes = jnp.where(first, even, odd) + pltpu.roll(jnp.where(first, odd, even), SUB - bit, 1)
    return planes.reshape(planes.shape[0] * SUB, LANES)


def kernel(
    light_count, view_count, density_hbm, albedo_hbm, color_hbm, shift_hbm, flip_hbm, out_ref,
    density, albedo, color, lateral, flips, ahead_of, tinted, totals, entered, received, cross_in, cross_out,
    part, part_total, swap, swap_total, comb, comb_total, got, got_total, rows4,
    load_sem, exit_send, exit_recv, core_send, core_recv, z_send, z_recv,
):
    slices, cells, columns = density.shape
    lights = color.shape[1]
    z_count = view_count // 2
    stages = light_count.bit_length() - 1
    chunks = columns // LANES
    rows = got.shape[3]
    per_slice = chunks // rows
    light_step = LIGHT_DEPTH / (slices * light_count)
    view_step = VIEW_DEPTH / (cells * view_count)

    loads = [
        pltpu.make_async_copy(density_hbm.at[x], density.at[x], load_sem.at[x]) for x in range(slices)
    ] + [
        pltpu.make_async_copy(src, dst, load_sem.at[slices + i])
        for i, (src, dst) in enumerate(
            ((flip_hbm, flips), (albedo_hbm, albedo), (shift_hbm, lateral), (color_hbm, color))
        )
    ]
    for load in loads:
        load.start()

    me_light = lax.axis_index("light")
    me_view = lax.axis_index("view")
    core = lax.rem(me_view, 2)
    z = lax.div(me_view, 2)
    other = 1 - core

    def partner(b):
        bit = lax.rem(lax.div(me_light, 2**b), 2)
        return me_light + (1 - 2 * bit) * 2**b

    barrier = pltpu.get_barrier_semaphore()
    for b in range(stages):
        pl.semaphore_signal(barrier, inc=1, device_id=(partner(b), me_view), device_id_type=MESH)
    pl.semaphore_signal(barrier, inc=1, device_id=(me_light, z * 2 + other), device_id_type=MESH)
    for step in range(1, z_count):
        pl.semaphore_signal(barrier, inc=1, device_id=(me_light, lax.rem(z + step, z_count) * 2 + core), device_id_type=MESH)

    ones = jnp.ones((chunks, cells, LANES), jnp.float32)
    chain = [ones] * 3
    for x in range(slices):
        loads[x].wait()
        ext = jnp.exp(-chunked(density[x]) * light_step)
        for a, amount in enumerate(SHIFTS):
            ahead_of[a, x] = chain[a]
            chain[a] = slide(chain[a] * ext, amount, 1.0)
    for a in range(3):
        totals[a, 0] = chain[a]
        entered[a] = ones

    pl.semaphore_wait(barrier, stages + 1 + z_count - 1)

    def facts(b):
        bit = lax.rem(lax.div(me_light, 2**b), 2)
        upward = lax.div(me_light, 2 ** (b + 1)) != light_count // 2 ** (b + 1) - 1
        return bit, upward

    def exit_copy(a, b):
        return pltpu.make_async_remote_copy(
            src_ref=totals.at[a, b, low], dst_ref=received.at[a, b, low],
            send_sem=exit_send.at[a, b], recv_sem=exit_recv.at[a, b],
            device_id=(partner(b), me_view), device_id_type=MESH,
        )

    half = chunks // 2
    crossed = stages == 2 and chunks % 2 == 0 and 3 * slices <= LANES
    reach = half + 1 if crossed else chunks
    low = pl.ds(0, reach)
    high = pl.ds(chunks - reach, reach)

    def cross_copy(a, b):
        return pltpu.make_async_remote_copy(
            src_ref=totals.at[a, 0, high] if b == 0 else cross_out.at[a], dst_ref=cross_in.at[a, b],
            send_sem=exit_send.at[a, stages + b], recv_sem=exit_recv.at[a, stages + b],
            device_id=(partner(1 - b), me_view), device_id_type=MESH,
        )

    def cross_first(a):
        @pl.when(me_light < 2)
        def _():
            cross_copy(a, 0).start()

        @pl.when(me_light == 0)
        def _():
            cross_out[a] = totals[a, 0, high]
            cross_copy(a, 1).start()

    def cross_second(a):
        @pl.when(me_light >= 2)
        def _():
            cross_copy(a, 0).wait_recv()
            came = cross_in[a, 0]
            joined = slide(came, SHIFTS[a] * slices * 2, 1.0) * totals[a, 0, high]
            cross_out[a] = jnp.where(me_light == 2, joined, came)
            cross_copy(a, 1).start()

    def cross_end(a):
        @pl.when(me_light >= 1)
        def _():
            cross_copy(a, 1).wait_recv()
            entered[a, half:] = cross_in[a, 1, 1:]

        @pl.when(me_light >= 2)
        def _():
            moved = slide(cross_in[a, 0], SHIFTS[a] * slices, 1.0) * cross_in[a, 1]
            entered[a, half:] = moved[1:]

    def cross_drain(a):
        @pl.when(me_light < 2)
        def _():
            cross_copy(a, 0).wait_send()

        @pl.when(me_light != 1)
        def _():
            cross_copy(a, 1).wait_send()

    def send_exit(a, b):
        bit, upward = facts(b)

        @pl.when((bit == 0) | upward)
        def _():
            exit_copy(a, b).start()

    def advance(a, b):
        amount = SHIFTS[a]
        bit, upward = facts(b)

        @pl.when((bit == 1) | upward)
        def _():
            exit_copy(a, b).wait_recv()

        @pl.when(bit == 1)
        def _():
            moved = received[a, b, low]
            for k in range(b):
                inner = lax.rem(lax.div(me_light, 2**k), 2)
                moved = jnp.where(inner == 1, slide(moved, amount * slices * 2**k, 1.0), moved)
            entered[a, low] = moved * entered[a, low]

        if b + 1 < stages:

            @pl.when(upward)
            def _():
                mine, theirs = totals[a, b, low], received[a, b, low]
                lower = jnp.where(bit == 1, theirs, mine)
                upper = jnp.where(bit == 1, mine, theirs)
                totals[a, b + 1, low] = slide(lower, amount * slices * 2**b, 1.0) * upper

            send_exit(a, b + 1)

    for a in range(3):
        send_exit(a, 0)
        if crossed:
            cross_first(a)

    def forward(a):
        for b in range(stages - 1):
            advance(a, b)
        if crossed:
            cross_second(a)

    loads[slices].wait()
    loads[slices + 1].wait()
    cell = lax.broadcasted_iota(jnp.int32, (chunks, cells, LANES), 1)
    for x in range(slices):
        depth = chunked(density[x]) * view_step
        running = depth
        for step in (1, 2, 4):
            running = running + jnp.where(cell >= step, pltpu.roll(running, step, 1), 0.0)
        column = jnp.broadcast_to(running[:, cells - 1 :, :], running.shape)
        ahead = jnp.where(flips[x] == 1, column - running, running - depth)
        weight = jnp.exp(-ahead) * (1.0 - jnp.exp(-depth))
        for c in range(3):
            tinted[c, x] = weight * chunked(albedo[c, x].astype(jnp.float32))
        total = column_sums(depth)
        for j in range(per_slice):
            piece = x * per_slice + j
            part_total[piece % 2, piece // 2] = total[j * rows : (j + 1) * rows]
        for a in range(3):
            if x + 1 == slices - (2 - a) * slices // 4:
                forward(a)

    def core_copy(src, dst, index):
        return pltpu.make_async_remote_copy(
            src_ref=src, dst_ref=dst, send_sem=core_send.at[index], recv_sem=core_recv.at[index],
            device_id=(me_light, z * 2 + other), device_id_type=MESH,
        )

    total_swap = core_copy(part_total.at[other], swap_total, 3)
    total_swap.start()

    def z_copy(src, dst, index, step):
        return pltpu.make_async_remote_copy(
            src_ref=src, dst_ref=dst, send_sem=z_send.at[index, step], recv_sem=z_recv.at[index, z],
            device_id=(me_light, lax.rem(z + step, z_count) * 2 + core), device_id_type=MESH,
        )

    def z_wait(dst, index, step):
        source = lax.rem(z + step, z_count)
        pltpu.make_async_remote_copy(
            src_ref=dst.at[source], dst_ref=dst.at[source], send_sem=z_send.at[index, step],
            recv_sem=z_recv.at[index, source], device_id=(me_light, source * 2 + core), device_id_type=MESH,
        ).wait_recv()

    def flip_of(piece):
        return flips[lax.div(piece, per_slice)]

    sends = []
    swaps = []

    def share_totals():
        total_swap.wait_recv()
        comb_total[...] = part_total[core] + swap_total[...]
        for step in range(1, z_count):
            copy = z_copy(comb_total.at[lax.rem(z + step, z_count)], got_total.at[z], 3, step)
            copy.start()
            sends.append(copy)
        got_total[z] = comb_total[z]
        for target in range(z_count):
            mine_first = flip_of(target * 2 + core) == core
            mine, theirs = part_total[core, target], swap_total[target]
            part_total[core, target] = jnp.where(mine_first, 1.0, jnp.exp(-theirs))
            swap_total[target] = jnp.where(mine_first, jnp.exp(-mine), 1.0)

    def render(a, wanted):
        entering = entered[a]
        for x in wanted:
            trans = slide(entering, SHIFTS[a] * x, 1.0) * ahead_of[a, x]
            for c in range(3):
                sums = column_sums(trans * tinted[c, x])
                for j in range(per_slice):
                    piece = x * per_slice + j
                    part[a, piece % 2, piece // 2, c] = sums[j * rows : (j + 1) * rows]

    def render_half(a, own):
        for parity in range(2):

            @pl.when((core if own else other) == parity)
            def _():
                render(a, range(parity, slices, 2))

    def march(a):
        if per_slice == 1:
            render_half(a, False)
        else:
            render(a, range(slices))
        copy = core_copy(part.at[a, other], swap.at[a], a)
        copy.start()
        swaps.append(copy)
        if a > 0:
            finish_swap(a - 1)
        if per_slice == 1:
            render_half(a, True)

    def finish_swap(a):
        swaps[a].wait_recv()
        for target in range(z_count):
            mine_fade, their_fade = part_total[core, target], swap_total[target]
            for c in range(3):
                comb[a, target, c] = mine_fade * part[a, core, target, c] + their_fade * swap[a, target, c]
        for step in range(1, z_count):
            copy = z_copy(comb.at[a, lax.rem(z + step, z_count)], got.at[a, z], a, step)
            copy.start()
            sends.append(copy)
        got[a, z] = comb[a, z]

    share_totals()
    for a in range(3):
        if stages:
            advance(a, stages - 1)
        if crossed:
            cross_end(a)
        march(a)
    finish_swap(2)

    loads[slices + 2].wait()
    loads[slices + 3].wait()
    for step in range(1, z_count):
        z_wait(got_total, 3, step)
    flip = flip_of(me_view)
    before = jnp.zeros(got_total.shape[1:], jnp.float32)
    fades = []
    for source in range(z_count):
        fades.append(before)
        before = before + got_total[source]
    for source in range(z_count):
        depth = jnp.where(flip == 1, before - fades[source] - got_total[source], fades[source])
        fades[source] = jnp.exp(-depth)
    opacity = 1.0 - jnp.exp(-before)
    for a in range(3):
        for step in range(1, z_count):
            z_wait(got.at[a], a, step)
        for c in range(3):
            value = fades[0] * got[a, 0, c]
            for source in range(1, z_count):
                value = value + fades[source] * got[a, source, c]
            rows4[a, pl.ds(c, rows, stride=4), :] = value
        rows4[a, pl.ds(3, rows, stride=4), :] = opacity
    field = lax.rem(lax.broadcasted_iota(jnp.int32, rows4.shape[1:], 0), 4)
    for light in range(lights):
        step = lateral[light]
        picked = jnp.where(step == SHIFTS[2], rows4[2], jnp.where(step == SHIFTS[0], rows4[0], rows4[1]))
        tint = jnp.where(
            field == 0, color[0, light], jnp.where(field == 1, color[1, light], jnp.where(field == 2, color[2, light], 1.0))
        )
        lit = picked * tint
        for r in range(rows):
            out_ref[light, :, r * LANES : (r + 1) * LANES] = lit[r * 4 : (r + 1) * 4, :]

    for copy in sends:
        copy.wait_send()
    for copy in swaps:
        copy.wait_send()
    total_swap.wait_send()
    for b in range(stages):
        bit, upward = facts(b)

        @pl.when((bit == 0) | upward)
        def _():
            for a in range(3):
                exit_copy(a, b).wait_send()
    if crossed:
        for a in range(3):
            cross_drain(a)


def local(density, albedo, light_color, light_shift, view_flip):
    slices, cells, columns = density.shape
    lights = light_shift.shape[0]
    light_count = lax.axis_size("light")
    view_count = lax.axis_size("view")
    z_count = view_count // 2
    stages = light_count.bit_length() - 1
    chunks = columns // LANES
    piece = slices * columns // view_count
    rows = piece // LANES
    f32 = jnp.float32
    anywhere = pl.BlockSpec(memory_space=pl.ANY)
    dma = pltpu.SemaphoreType.DMA
    return pl.pallas_call(
        functools.partial(kernel, light_count, view_count),
        out_shape=jax.ShapeDtypeStruct((lights, 4, piece), f32),
        in_specs=[anywhere] * 5,
        out_specs=pl.BlockSpec(memory_space=pltpu.VMEM),
        scratch_shapes=[
            pltpu.VMEM(density.shape, f32),
            pltpu.VMEM(albedo.shape, albedo.dtype),
            pltpu.SMEM((3, lights), f32),
            pltpu.SMEM((lights,), jnp.int32),
            pltpu.SMEM((slices,), jnp.int32),
            pltpu.VMEM((3, slices, chunks, cells, LANES), f32),
            pltpu.VMEM((3, slices, chunks, cells, LANES), f32),
            pltpu.VMEM((3, stages, chunks, cells, LANES), f32),
            pltpu.VMEM((3, chunks, cells, LANES), f32),
            pltpu.VMEM((3, stages, chunks, cells, LANES), f32),
            pltpu.VMEM((3, 2, chunks // 2 + 1, cells, LANES), f32),
            pltpu.VMEM((3, chunks // 2 + 1, cells, LANES), f32),
            pltpu.VMEM((3, 2, z_count, 3, rows, LANES), f32),
            pltpu.VMEM((2, z_count, rows, LANES), f32),
            pltpu.VMEM((3, z_count, 3, rows, LANES), f32),
            pltpu.VMEM((z_count, rows, LANES), f32),
            pltpu.VMEM((3, z_count, 3, rows, LANES), f32),
            pltpu.VMEM((z_count, rows, LANES), f32),
            pltpu.VMEM((3, z_count, 3, rows, LANES), f32),
            pltpu.VMEM((z_count, rows, LANES), f32),
            pltpu.VMEM((3, rows * 4, LANES), f32),
            dma((slices + 4,)),
            dma((3, stages + 2)),
            dma((3, stages + 2)),
            dma((4,)),
            dma((4,)),
            dma((4, z_count)),
            dma((4, z_count)),
        ],
        compiler_params=pltpu.CompilerParams(
            collective_id=0, has_side_effects=True, vmem_limit_bytes=32 * 2**20
        ),
    )(*(pltpu.with_memory_space_constraint(x, pltpu.HBM) for x in (density, albedo, light_color.T, light_shift, view_flip)))


def solution(mesh):
    return jax.shard_map(
        local,
        mesh=mesh,
        in_specs=(P("light", "view", None), P(None, "light", "view", None), P(), P(), P("light")),
        out_specs=P(None, None, ("light", "view")),
        check_vma=False,
    )
```

```python
import functools
import jax
import jax.numpy as jnp
from jax import lax
from jax.experimental import pallas as pl
from jax.experimental.pallas import tpu as pltpu
from jax.sharding import PartitionSpec as P

LIGHT_DEPTH = 1.5
VIEW_DEPTH = 2.0
LANES = 128
SUB = 8
SHIFTS = (-1, 0, 1)
MESH = pl.DeviceIdType.MESH


def chunked(plane):
    return jnp.stack([plane[:, k : k + LANES] for k in range(0, plane.shape[1], LANES)])


def slide(planes, amount, fill):
    if amount == 0:
        return planes
    count = planes.shape[0]
    whole, part = divmod(abs(amount), LANES)
    whole = min(whole, count)
    lane = lax.broadcasted_iota(jnp.int32, planes.shape, 2)

    def blocks(n):
        return [jnp.full((n,) + planes.shape[1:], fill, planes.dtype)] if n else []

    if amount > 0:
        if whole:
            planes = jnp.concatenate(blocks(whole) + [planes[: count - whole]] * (whole < count), axis=0)
        if part:
            turned = pltpu.roll(planes, part, 2)
            before = jnp.concatenate(blocks(1) + [turned[:-1]], axis=0)
            planes = jnp.where(lane < part, before, turned)
    else:
        if whole:
            planes = jnp.concatenate([planes[whole:]] * (whole < count) + blocks(whole), axis=0)
        if part:
            turned = pltpu.roll(planes, LANES - part, 2)
            after = jnp.concatenate([turned[1:]] + blocks(1), axis=0)
            planes = jnp.where(lane >= LANES - part, after, turned)
    return planes


def column_sums(planes):
    for bit in (1, 2, 4):
        pairs = planes.reshape(planes.shape[0] // 2, 2, SUB, LANES)
        even, odd = pairs[:, 0], pairs[:, 1]
        row = lax.broadcasted_iota(jnp.int32, even.shape, 1)
        first = (row & bit) == 0
        planes = jnp.where(first, even, odd) + pltpu.roll(jnp.where(first, odd, even), SUB - bit, 1)
    return planes.reshape(planes.shape[0] * SUB, LANES)


def kernel(
    light_count, view_count, density_hbm, albedo_hbm, color_hbm, shift_hbm, flip_hbm, out_ref,
    density, albedo, color, lateral, flips, ahead_of, tinted, totals, entered, received, cross_in, cross_out,
    part, part_total, swap, swap_total, comb, comb_total, got, got_total, rows4,
    load_sem, exit_send, exit_recv, core_send, core_recv, z_send, z_recv,
):
    slices, cells, columns = density.shape
    lights = color.shape[1]
    z_count = view_count // 2
    stages = light_count.bit_length() - 1
    chunks = columns // LANES
    rows = got.shape[3]
    per_slice = chunks // rows
    light_step = LIGHT_DEPTH / (slices * light_count)
    view_step = VIEW_DEPTH / (cells * view_count)

    loads = [
        pltpu.make_async_copy(density_hbm.at[x], density.at[x], load_sem.at[x]) for x in range(slices)
    ] + [
        pltpu.make_async_copy(src, dst, load_sem.at[slices + i])
        for i, (src, dst) in enumerate(
            ((flip_hbm, flips), (albedo_hbm, albedo), (shift_hbm, lateral), (color_hbm, color))
        )
    ]
    for load in loads:
        load.start()

    me_light = lax.axis_index("light")
    me_view = lax.axis_index("view")
    core = lax.rem(me_view, 2)
    z = lax.div(me_view, 2)
    other = 1 - core

    def partner(b):
        bit = lax.rem(lax.div(me_light, 2**b), 2)
        return me_light + (1 - 2 * bit) * 2**b

    barrier = pltpu.get_barrier_semaphore()
    for b in range(stages):
        pl.semaphore_signal(barrier, inc=1, device_id=(partner(b), me_view), device_id_type=MESH)
    pl.semaphore_signal(barrier, inc=1, device_id=(me_light, z * 2 + other), device_id_type=MESH)
    for step in range(1, z_count):
        pl.semaphore_signal(barrier, inc=1, device_id=(me_light, lax.rem(z + step, z_count) * 2 + core), device_id_type=MESH)

    ones = jnp.ones((chunks, cells, LANES), jnp.float32)
    chain = [ones] * 3
    for x in range(slices):
        loads[x].wait()
        ext = jnp.exp(-chunked(density[x]) * light_step)
        for a, amount in enumerate(SHIFTS):
            ahead_of[a, x] = chain[a]
            chain[a] = slide(chain[a] * ext, amount, 1.0)
    for a in range(3):
        totals[a, 0] = chain[a]
        entered[a] = ones

    pl.semaphore_wait(barrier, stages + 1 + z_count - 1)

    def facts(b):
        bit = lax.rem(lax.div(me_light, 2**b), 2)
        upward = lax.div(me_light, 2 ** (b + 1)) != light_count // 2 ** (b + 1) - 1
        return bit, upward

    def exit_copy(a, b):
        return pltpu.make_async_remote_copy(
            src_ref=totals.at[a, b, low], dst_ref=received.at[a, b, low],
            send_sem=exit_send.at[a, b], recv_sem=exit_recv.at[a, b],
            device_id=(partner(b), me_view), device_id_type=MESH,
        )

    half = chunks // 2
    crossed = stages == 2 and chunks % 2 == 0 and 3 * slices <= LANES
    reach = half + 1 if crossed else chunks
    low = pl.ds(0, reach)
    high = pl.ds(chunks - reach, reach)

    def cross_copy(a, b):
        return pltpu.make_async_remote_copy(
            src_ref=totals.at[a, 0, high] if b == 0 else cross_out.at[a], dst_ref=cross_in.at[a, b],
            send_sem=exit_send.at[a, stages + b], recv_sem=exit_recv.at[a, stages + b],
            device_id=(partner(1 - b), me_view), device_id_type=MESH,
        )

    def cross_first(a):
        @pl.when(me_light < 2)
        def _():
            cross_copy(a, 0).start()

    def cross_second(a):
        @pl.when(me_light == 0)
        def _():
            cross_out[a] = totals[a, 0, high]
            cross_copy(a, 1).start()

        @pl.when(me_light >= 2)
        def _():
            cross_copy(a, 0).wait_recv()
            came = cross_in[a, 0]
            joined = slide(came, SHIFTS[a] * slices * 2, 1.0) * totals[a, 0, high]
            cross_out[a] = jnp.where(me_light == 2, joined, came)
            cross_copy(a, 1).start()

    def cross_end(a):
        @pl.when(me_light >= 1)
        def _():
            cross_copy(a, 1).wait_recv()
            entered[a, half:] = cross_in[a, 1, 1:]

        @pl.when(me_light >= 2)
        def _():
            moved = slide(cross_in[a, 0], SHIFTS[a] * slices, 1.0) * cross_in[a, 1]
            entered[a, half:] = moved[1:]

    def cross_drain(a):
        @pl.when(me_light < 2)
        def _():
            cross_copy(a, 0).wait_send()

        @pl.when(me_light != 1)
        def _():
            cross_copy(a, 1).wait_send()

    def send_exit(a, b):
        bit, upward = facts(b)

        @pl.when((bit == 0) | upward)
        def _():
            exit_copy(a, b).start()

    def advance(a, b):
        amount = SHIFTS[a]
        bit, upward = facts(b)

        @pl.when((bit == 1) | upward)
        def _():
            exit_copy(a, b).wait_recv()

        @pl.when(bit == 1)
        def _():
            moved = received[a, b, low]
            for k in range(b):
                inner = lax.rem(lax.div(me_light, 2**k), 2)
                moved = jnp.where(inner == 1, slide(moved, amount * slices * 2**k, 1.0), moved)
            entered[a, low] = moved * entered[a, low]

        if b + 1 < stages:

            @pl.when(upward)
            def _():
                mine, theirs = totals[a, b, low], received[a, b, low]
                lower = jnp.where(bit == 1, theirs, mine)
                upper = jnp.where(bit == 1, mine, theirs)
                totals[a, b + 1, low] = slide(lower, amount * slices * 2**b, 1.0) * upper

            send_exit(a, b + 1)

    for a in range(3):
        send_exit(a, 0)
        if crossed:
            cross_first(a)

    loads[slices].wait()
    loads[slices + 1].wait()
    cell = lax.broadcasted_iota(jnp.int32, (chunks, cells, LANES), 1)
    for x in range(slices):
        depth = chunked(density[x]) * view_step
        running = depth
        for step in (1, 2, 4):
            running = running + jnp.where(cell >= step, pltpu.roll(running, step, 1), 0.0)
        column = jnp.broadcast_to(running[:, cells - 1 :, :], running.shape)
        ahead = jnp.where(flips[x] == 1, column - running, running - depth)
        weight = jnp.exp(-ahead) * (1.0 - jnp.exp(-depth))
        for c in range(3):
            tinted[c, x] = weight * chunked(albedo[c, x].astype(jnp.float32))
        total = column_sums(depth)
        for j in range(per_slice):
            piece = x * per_slice + j
            part_total[piece % 2, piece // 2] = total[j * rows : (j + 1) * rows]

    def core_copy(src, dst, index):
        return pltpu.make_async_remote_copy(
            src_ref=src, dst_ref=dst, send_sem=core_send.at[index], recv_sem=core_recv.at[index],
            device_id=(me_light, z * 2 + other), device_id_type=MESH,
        )

    total_swap = core_copy(part_total.at[other], swap_total, 3)
    total_swap.start()

    def z_copy(src, dst, index, step):
        return pltpu.make_async_remote_copy(
            src_ref=src, dst_ref=dst, send_sem=z_send.at[index, step], recv_sem=z_recv.at[index, z],
            device_id=(me_light, lax.rem(z + step, z_count) * 2 + core), device_id_type=MESH,
        )

    def z_wait(dst, index, step):
        source = lax.rem(z + step, z_count)
        pltpu.make_async_remote_copy(
            src_ref=dst.at[source], dst_ref=dst.at[source], send_sem=z_send.at[index, step],
            recv_sem=z_recv.at[index, source], device_id=(me_light, source * 2 + core), device_id_type=MESH,
        ).wait_recv()

    def flip_of(piece):
        return flips[lax.div(piece, per_slice)]

    sends = []
    swaps = []

    def share_totals():
        total_swap.wait_recv()
        comb_total[...] = part_total[core] + swap_total[...]
        for step in range(1, z_count):
            copy = z_copy(comb_total.at[lax.rem(z + step, z_count)], got_total.at[z], 3, step)
            copy.start()
            sends.append(copy)
        got_total[z] = comb_total[z]
        for target in range(z_count):
            mine_first = flip_of(target * 2 + core) == core
            mine, theirs = part_total[core, target], swap_total[target]
            part_total[core, target] = jnp.where(mine_first, 1.0, jnp.exp(-theirs))
            swap_total[target] = jnp.where(mine_first, jnp.exp(-mine), 1.0)

    def march(a):
        entering = entered[a]
        for x in range(slices):
            trans = slide(entering, SHIFTS[a] * x, 1.0) * ahead_of[a, x]
            for c in range(3):
                sums = column_sums(trans * tinted[c, x])
                for j in range(per_slice):
                    piece = x * per_slice + j
                    part[a, piece % 2, piece // 2, c] = sums[j * rows : (j + 1) * rows]
        copy = core_copy(part.at[a, other], swap.at[a], a)
        copy.start()
        swaps.append(copy)

    def finish_swap(a):
        swaps[a].wait_recv()
        for target in range(z_count):
            mine_fade, their_fade = part_total[core, target], swap_total[target]
            for c in range(3):
                comb[a, target, c] = mine_fade * part[a, core, target, c] + their_fade * swap[a, target, c]
        for step in range(1, z_count):
            copy = z_copy(comb.at[a, lax.rem(z + step, z_count)], got.at[a, z], a, step)
            copy.start()
            sends.append(copy)
        got[a, z] = comb[a, z]

    for b in range(stages - 1):
        for a in range(3):
            advance(a, b)
            if crossed:
                cross_second(a)
    share_totals()
    for a in range(3):
        if stages:
            advance(a, stages - 1)
        if crossed:
            cross_end(a)
        march(a)
        if a > 0:
            finish_swap(a - 1)
    finish_swap(2)

    loads[slices + 2].wait()
    loads[slices + 3].wait()
    for step in range(1, z_count):
        z_wait(got_total, 3, step)
    flip = flip_of(me_view)
    before = jnp.zeros(got_total.shape[1:], jnp.float32)
    fades = []
    for source in range(z_count):
        fades.append(before)
        before = before + got_total[source]
    for source in range(z_count):
        depth = jnp.where(flip == 1, before - fades[source] - got_total[source], fades[source])
        fades[source] = jnp.exp(-depth)
    opacity = 1.0 - jnp.exp(-before)
    for a in range(3):
        for step in range(1, z_count):
            z_wait(got.at[a], a, step)
        for c in range(3):
            value = fades[0] * got[a, 0, c]
            for source in range(1, z_count):
                value = value + fades[source] * got[a, source, c]
            rows4[a, pl.ds(c, rows, stride=4), :] = value
        rows4[a, pl.ds(3, rows, stride=4), :] = opacity
    field = lax.rem(lax.broadcasted_iota(jnp.int32, rows4.shape[1:], 0), 4)
    for light in range(lights):
        step = lateral[light]
        picked = jnp.where(step == SHIFTS[2], rows4[2], jnp.where(step == SHIFTS[0], rows4[0], rows4[1]))
        tint = jnp.where(
            field == 0, color[0, light], jnp.where(field == 1, color[1, light], jnp.where(field == 2, color[2, light], 1.0))
        )
        lit = picked * tint
        for r in range(rows):
            out_ref[light, :, r * LANES : (r + 1) * LANES] = lit[r * 4 : (r + 1) * 4, :]

    for copy in sends:
        copy.wait_send()
    for copy in swaps:
        copy.wait_send()
    total_swap.wait_send()
    for b in range(stages):
        bit, upward = facts(b)

        @pl.when((bit == 0) | upward)
        def _():
            for a in range(3):
                exit_copy(a, b).wait_send()
    if crossed:
        for a in range(3):
            cross_drain(a)


def local(density, albedo, light_color, light_shift, view_flip):
    slices, cells, columns = density.shape
    lights = light_shift.shape[0]
    light_count = lax.axis_size("light")
    view_count = lax.axis_size("view")
    z_count = view_count // 2
    stages = light_count.bit_length() - 1
    chunks = columns // LANES
    piece = slices * columns // view_count
    rows = piece // LANES
    f32 = jnp.float32
    anywhere = pl.BlockSpec(memory_space=pl.ANY)
    dma = pltpu.SemaphoreType.DMA
    return pl.pallas_call(
        functools.partial(kernel, light_count, view_count),
        out_shape=jax.ShapeDtypeStruct((lights, 4, piece), f32),
        in_specs=[anywhere] * 5,
        out_specs=pl.BlockSpec(memory_space=pltpu.VMEM),
        scratch_shapes=[
            pltpu.VMEM(density.shape, f32),
            pltpu.VMEM(albedo.shape, albedo.dtype),
            pltpu.SMEM((3, lights), f32),
            pltpu.SMEM((lights,), jnp.int32),
            pltpu.SMEM((slices,), jnp.int32),
            pltpu.VMEM((3, slices, chunks, cells, LANES), f32),
            pltpu.VMEM((3, slices, chunks, cells, LANES), f32),
            pltpu.VMEM((3, stages, chunks, cells, LANES), f32),
            pltpu.VMEM((3, chunks, cells, LANES), f32),
            pltpu.VMEM((3, stages, chunks, cells, LANES), f32),
            pltpu.VMEM((3, 2, chunks // 2 + 1, cells, LANES), f32),
            pltpu.VMEM((3, chunks // 2 + 1, cells, LANES), f32),
            pltpu.VMEM((3, 2, z_count, 3, rows, LANES), f32),
            pltpu.VMEM((2, z_count, rows, LANES), f32),
            pltpu.VMEM((3, z_count, 3, rows, LANES), f32),
            pltpu.VMEM((z_count, rows, LANES), f32),
            pltpu.VMEM((3, z_count, 3, rows, LANES), f32),
            pltpu.VMEM((z_count, rows, LANES), f32),
            pltpu.VMEM((3, z_count, 3, rows, LANES), f32),
            pltpu.VMEM((z_count, rows, LANES), f32),
            pltpu.VMEM((3, rows * 4, LANES), f32),
            dma((slices + 4,)),
            dma((3, stages + 2)),
            dma((3, stages + 2)),
            dma((4,)),
            dma((4,)),
            dma((4, z_count)),
            dma((4, z_count)),
        ],
        compiler_params=pltpu.CompilerParams(
            collective_id=0, has_side_effects=True, vmem_limit_bytes=32 * 2**20
        ),
    )(*(pltpu.with_memory_space_constraint(x, pltpu.HBM) for x in (density, albedo, light_color.T, light_shift, view_flip)))


def solution(mesh):
    return jax.shard_map(
        local,
        mesh=mesh,
        in_specs=(P("light", "view", None), P(None, "light", "view", None), P(), P(), P("light")),
        out_specs=P(None, None, ("light", "view")),
        check_vma=False,
    )
```
